32 devices in a mesh: dom: 4 (over x, core), mem: 8 (over z, y).
Axes of the slice: x: 2, y: 2, z: 4, core: 2. Of those that a mesh axis runs over, the one named last changes fastest.
Arguments:
- background_trajectories: bfloat16 [512, 98304], P('mem', 'dom'), may hold values from -6 to 6
- jittered_measurement: bfloat16 [512, 98304], P('mem', 'dom'), may hold values from -6 to 6
- measurement_inverse_variance: float32 [98304], P('dom'), may hold values from 0.25 to 4
- measured_point_number: int32 [1536], P('dom'), may hold values from 0 to 64
- adjacent_region_list: int32 [1536, 16], P(('dom', 'mem')), may hold values from 0 to 1535, as said below
- nearby_separation_tier: int32 [1536, 16], P(('dom', 'mem')), may hold values from 0 to 7, as said below
Outputs:
- increment: bfloat16 [512, 98304], P('mem', 'dom')
The draws below stay inside these ranges and needn't reach their ends.
Inputs may be any that keep to these rules, and one draw needn't show every extreme that they name: Cells 0 to measured_point_number[p] - 1 of patch p are the observed ones. `adjacent_region_list`: column 0 of row p is p itself. The other 15 entries are distinct patches (p + o) mod 1536 with 0 < |o| <= 16, and every row holds both o = -16 and o = 16. `nearby_separation_tier`: column 0 is 0; the other columns hold 1 to 7.
All inputs are finite; a program needn't handle non-finite values.
Results may differ from the reference program's by a relative error of at most 0.0059.
Values may be sent and summed in bfloat16 or wider, within the bound.
No kernel may reach another device: no remote copies, remote signals or barrier semaphores. Data moves between devices by JAX's collectives and lax.ppermute only.
A program may use at most 128 MiB of HBM per device.

```python
import math
import jax
import jax.numpy as jnp
from jax import lax

MEMBER_TOTAL = 512
PC = 64
REACH = 16
NB = 16
NCLASS = 8
NPATCH = 1536
GRID_POINTS = 98304


def neighbour_table(base_key):
    row_keys = jax.random.split(jax.random.fold_in(base_key, 11), NPATCH)
    inside = jnp.concatenate([jnp.arange(-REACH + 1, 0, dtype=jnp.int32), jnp.arange(1, REACH, dtype=jnp.int32)])

    def one_row(row_key):
        first_key, latter_seed_handle = jax.random.split(row_key)
        chosen = jax.random.permutation(first_key, inside)[:NB - 3]
        offsets = jnp.concatenate([jnp.array([-REACH, REACH], dtype=jnp.int32), chosen])
        offsets = jax.random.permutation(latter_seed_handle, offsets)
        return jnp.concatenate([jnp.zeros((1,), jnp.int32), offsets])
    every_shift_amount = jax.vmap(one_row)(row_keys)
    return (jnp.arange(NPATCH, dtype=jnp.int32)[:, None] + every_shift_amount) % NPATCH


def draw_adjacent_region_list(key, part):
    return neighbour_table(key).astype(jnp.int32)


def draw_nearby_separation_tier(key, part):
    classes = jax.random.randint(jax.random.fold_in(key, 23), (NPATCH, NB - 1), 1, NCLASS, dtype=jnp.int32)
    return jnp.concatenate([jnp.zeros((NPATCH, 1), jnp.int32), classes], axis=1)


def plant(values, own_key, least, largest):
    longest = values.shape.index(max(values.shape))
    spots = []
    for shift in (0, 1):
        where = [jax.random.randint(jax.random.fold_in(own_key, axis), (), 0, length) for axis, length in enumerate(values.shape)]
        where[longest] = (where[longest] + shift) % values.shape[longest]
        spots.append(tuple(where))
    return values.at[spots[0]].set(least).at[spots[1]].set(largest)


def levels(rng, extent, cuts, low, top_value):
    def one(dim, blocks):
        heights = jax.random.uniform(jax.random.fold_in(jax.random.fold_in(rng, 6), dim), (blocks,), jnp.float32, low / len(cuts), top_value / len(cuts))
        return jnp.repeat(jnp.exp(heights), extent[dim] // blocks).reshape((-1,) + (1,) * (len(extent) - dim - 1))

    level = one(*cuts[0])
    for cut in cuts[1:]:
        level = level * one(*cut)
    return level


def bell_draw(rng, shape, width, most, pieces=(), kind=jnp.bfloat16):
    values = width * jax.random.normal(rng, shape, jnp.float32)
    if pieces:
        values = values * levels(rng, shape, pieces, -0.22, 0.18)
    return jnp.clip(values, -most, most).astype(kind)


def setup_inputs(seed: int = 0) -> dict:
    streams_of = jax.random.split(jax.random.key(seed), 7)
    background_trajectories = bell_draw(streams_of[0], (MEMBER_TOTAL, GRID_POINTS), 1.0, 6.0, ((0, 8), (1, 4)))
    jittered_measurement = bell_draw(streams_of[1], (MEMBER_TOTAL, GRID_POINTS), 1.0, 6.0, ((0, 8), (1, 4)))
    measurement_inverse_variance = jnp.clip(jnp.exp(math.log(4.0) - 2.7725887 * jax.random.uniform(streams_of[2], (GRID_POINTS,), jnp.float32) ** levels(streams_of[2], (GRID_POINTS,), ((0, 4),), -0.2, 0.2)), 0.25, 4.0)
    measured_point_number = plant(jax.random.randint(streams_of[3], (NPATCH,), 0, PC + 1), jax.random.fold_in(streams_of[3], 1), 0, PC).astype(jnp.int32)
    adjacent_region_list = draw_adjacent_region_list(jax.random.fold_in(streams_of[6], 71), 0)
    nearby_separation_tier = draw_nearby_separation_tier(jax.random.fold_in(streams_of[6], 71), 0)
    return dict(background_trajectories=background_trajectories, jittered_measurement=jittered_measurement, measurement_inverse_variance=measurement_inverse_variance, measured_point_number=measured_point_number, adjacent_region_list=adjacent_region_list, nearby_separation_tier=nearby_separation_tier)


def gc_taper(taper_cutoff_length):
    return 1.0 - (5.0 / 3.0) * taper_cutoff_length ** 2 + 0.625 * taper_cutoff_length ** 3 + 0.5 * taper_cutoff_length ** 4 - 0.25 * taper_cutoff_length ** 5


def reference(background_trajectories, jittered_measurement, measurement_inverse_variance, measured_point_number, adjacent_region_list, nearby_separation_tier):
    observed = (jnp.arange(PC, dtype=jnp.int32)[None, :] < measured_point_number[:, None]).reshape(-1)
    measurement_gain_factor = jnp.where(observed, measurement_inverse_variance, jnp.float32(0.0))
    departure_residual = (measurement_gain_factor[None, :] * (jittered_measurement.astype(jnp.float32) - background_trajectories.astype(jnp.float32))).astype(jnp.bfloat16)
    sample_mean_state = jnp.mean(background_trajectories.astype(jnp.float32), axis=0)
    random_jitter_draws = (background_trajectories.astype(jnp.float32) - sample_mean_state[None, :]).astype(jnp.bfloat16)
    taper_weight = gc_taper(nearby_separation_tier.astype(jnp.float32) / NCLASS) / (MEMBER_TOTAL - 1)
    perturb_blocks = random_jitter_draws.reshape(MEMBER_TOTAL, NPATCH, PC)
    innov_blocks = departure_residual.reshape(MEMBER_TOTAL, NPATCH, PC)
    block_rows = math.gcd(NPATCH, 64)

    def block_update(first_patch):
        near_ids = lax.dynamic_slice_in_dim(adjacent_region_list, first_patch, block_rows, 0)
        near_weights = lax.dynamic_slice_in_dim(taper_weight, first_patch, block_rows, 0)
        own_cols = lax.dynamic_slice_in_dim(perturb_blocks, first_patch, block_rows, 1)
        near_cols = jnp.take(perturb_blocks, near_ids, axis=1)
        near_innov = jnp.take(innov_blocks, near_ids, axis=1)
        covariance = jnp.einsum("kbc,kbjd->bcjd", own_cols.astype(jnp.float32), near_cols.astype(jnp.float32))
        covariance = (covariance * near_weights[:, None, :, None]).astype(jnp.bfloat16)
        result_block = jnp.einsum("bcjd,kbjd->kbc", covariance.astype(jnp.float32), near_innov.astype(jnp.float32))
        return result_block.astype(jnp.bfloat16)

    starts = jnp.arange(0, NPATCH, block_rows, dtype=jnp.int32)
    blocks = lax.map(block_update, starts)
    return jnp.moveaxis(blocks, 0, 1).reshape(MEMBER_TOTAL, GRID_POINTS)
```

```python
import functools
import math

import jax
import jax.numpy as jnp
from jax import lax
from jax.experimental import pallas as pl
from jax.experimental.pallas import tpu as pltpu
from jax.sharding import PartitionSpec as P

PC = 64
REACH = 16
NCLASS = 8
AXES = ("dom", "mem")
CHUNK = REACH * PC
BLOCK = 256
BLOCK_PATCHES = BLOCK // PC
BLOCKS = CHUNK // BLOCK
WINDOW_PATCHES = BLOCK_PATCHES + 2 * REACH
VMEM_BYTES = 48 * 2**20


def gc_taper(taper_cutoff_length):
    return (
        1.0
        - 5.0 / 3.0 * taper_cutoff_length**2
        + 0.625 * taper_cutoff_length**3
        + 0.5 * taper_cutoff_length**4
        - 0.25 * taper_cutoff_length**5
    )


def gain_of(measurement_inverse_variance, measured_point_number):
    observed = (jnp.arange(PC, dtype=jnp.int32)[None, :] < measured_point_number[:, None]).reshape(
        -1
    )
    return jnp.where(observed, measurement_inverse_variance, jnp.float32(0.0))


def dense_weights(adjacent_region_list, nearby_separation_tier, all_members):
    rows = adjacent_region_list.shape[0]
    groups = lax.axis_size("mem")
    all_patches = rows * lax.axis_size("dom") * groups
    first = (lax.axis_index("dom") * groups + lax.axis_index("mem")) * rows
    own_ids = first + jnp.arange(rows, dtype=jnp.int32)[:, None]
    offset = (
        adjacent_region_list - own_ids + all_patches + all_patches // 2
    ) % all_patches - all_patches // 2
    weight = gc_taper(nearby_separation_tier.astype(jnp.float32) / NCLASS) / (all_members - 1)
    slots = jnp.arange(2 * REACH + 1, dtype=jnp.int32) - REACH
    return jnp.sum(
        jnp.where(offset[:, :, None] == slots[None, None, :], weight[:, :, None], 0.0), axis=1
    )


def source_kernel(place, bg1, jit1, gain1, bg2, jit2, gain2, piece1, piece2):
    rows = bg1.shape[0]
    for bg, jit, gain, piece in ((bg1, jit1, gain1, piece1), (bg2, jit2, gain2, piece2)):
        piece[pl.ds(0, rows), :] = bg[...]
        piece[pl.ds(rows, rows), :] = (
            gain[...] * (jit[...].astype(jnp.float32) - bg[...].astype(jnp.float32))
        ).astype(jnp.bfloat16)


def source_pieces(place, bg, jit, gain):
    n = place.shape[1]
    rows = bg.shape[0]

    def specs(piece):
        return [
            pl.BlockSpec((rows, CHUNK), lambda i, place: (0, place[piece, i])),
            pl.BlockSpec((rows, CHUNK), lambda i, place: (0, place[piece, i])),
            pl.BlockSpec((1, CHUNK), lambda i, place: (0, place[piece, i])),
        ]

    out = jax.ShapeDtypeStruct((2 * rows, n * CHUNK), jnp.bfloat16)
    return pl.pallas_call(
        source_kernel,
        grid_spec=pltpu.PrefetchScalarGridSpec(
            num_scalar_prefetch=1,
            grid=(n,),
            in_specs=specs(0) + specs(1),
            out_specs=[pl.BlockSpec((2 * rows, CHUNK), lambda i, place: (0, i))] * 2,
        ),
        out_shape=(out, out),
        cost_estimate=pl.CostEstimate(
            flops=8 * rows * n * CHUNK, bytes_accessed=16 * rows * n * CHUNK, transcendentals=0
        ),
        name="source_pieces",
    )(place, bg, jit, gain, bg, jit, gain)


def collect_kernel(first, second, states, innov):
    rows = first.shape[0] // 2
    for at, piece in ((0, first), (rows, second)):
        states[pl.ds(at, rows), :] = piece[pl.ds(0, rows), :]
        innov[pl.ds(at, rows), :] = piece[pl.ds(rows, rows), :]


def collect(first, second):
    n = first.shape[1] // CHUNK
    block = pl.BlockSpec((first.shape[0], CHUNK), lambda i: (0, i))
    return pl.pallas_call(
        collect_kernel,
        grid=(n,),
        in_specs=[block] * 2,
        out_specs=[block] * 2,
        out_shape=(jax.ShapeDtypeStruct(first.shape, first.dtype),) * 2,
        cost_estimate=pl.CostEstimate(flops=0, bytes_accessed=8 * first.size, transcendentals=0),
        name="collect",
    )(first, second)


def center_kernel(turn, own, innov, outer, outer_innov, cross, cross_outer, draws, innov_all):
    rows = own.shape[0] // 2
    low = pl.multiple_of(turn[0] * rows, rows)
    high = pl.multiple_of((1 - turn[0]) * rows, rows)
    members = 8 * rows
    for j in range(CHUNK // BLOCK):
        cells = pl.ds(j * BLOCK, BLOCK)
        parts = [
            ref[pl.ds(at, rows), cells].astype(jnp.float32)
            for ref in (own, outer, cross, cross_outer)
            for at in (low, high)
        ]
        total = functools.reduce(jnp.add, parts)
        mean = jnp.sum(total, axis=0, keepdims=True) / members
        perturb = jnp.concatenate([(part - mean).astype(jnp.bfloat16) for part in parts], axis=0)
        draws[cells, :] = perturb.T
    for at, ref in ((0, innov), (2 * rows, outer_innov)):
        innov_all[pl.ds(at, rows), :] = ref[pl.ds(low, rows), :]
        innov_all[pl.ds(at + rows, rows), :] = ref[pl.ds(high, rows), :]


def center(turn, number, own, innov, outer, outer_innov, cross, cross_outer):
    rows = own.shape[0] // 2
    block = pl.BlockSpec((2 * rows, CHUNK), lambda i: (0, number))
    return pl.pallas_call(
        center_kernel,
        grid=(1,),
        in_specs=[pl.BlockSpec(memory_space=pltpu.SMEM)] + [block] * 6,
        out_specs=[
            pl.BlockSpec((CHUNK, 8 * rows), lambda i: (0, 0)),
            pl.BlockSpec((4 * rows, CHUNK), lambda i: (0, 0)),
        ],
        out_shape=(
            jax.ShapeDtypeStruct((CHUNK, 8 * rows), jnp.bfloat16),
            jax.ShapeDtypeStruct((4 * rows, CHUNK), jnp.bfloat16),
        ),
        cost_estimate=pl.CostEstimate(
            flops=32 * rows * CHUNK, bytes_accessed=48 * rows * CHUNK, transcendentals=0
        ),
        compiler_params=pltpu.CompilerParams(vmem_limit_bytes=VMEM_BYTES),
        name="center",
    )(turn, own, innov, outer, outer_innov, cross, cross_outer)


def window_pieces(b):
    return [(0, b * BLOCK, CHUNK - b * BLOCK), (1, 0, CHUNK), (2, 0, (b + 1) * BLOCK)]


def update_kernel(n, turn, *refs):
    draws, innov = refs[: n + 2], refs[n + 2 : 2 * n + 4]
    weights, inner, outer, covariance = refs[2 * n + 4 :]
    rows = inner.shape[0] // 2
    low = pl.multiple_of(turn[0] * rows, rows)
    high = pl.multiple_of((1 - turn[0]) * rows, rows)

    def covariances(k):
        i, b = divmod(k, BLOCKS)
        own = draws[i + 1][pl.ds(b * BLOCK, BLOCK), :]
        done = 0
        for chunk, first, cells in window_pieces(b):
            patches = cells // PC
            product = lax.dot_general(
                draws[i + chunk][pl.ds(first, cells), :],
                own,
                (((1,), (1,)), ((), ())),
                preferred_element_type=jnp.float32,
            )
            weight = weights[k, pl.ds(done, patches), :]
            product = product.reshape(patches, PC, BLOCK) * weight[:, None, :]
            covariance[k % 2, pl.ds(done * PC, cells), :] = product.astype(jnp.bfloat16).reshape(
                cells, BLOCK
            )
            done += patches

    def increments(k):
        i, b = divmod(k, BLOCKS)
        total, done = None, 0
        for chunk, first, cells in window_pieces(b):
            term = jnp.dot(
                innov[i + chunk][:, pl.ds(first, cells)],
                covariance[k % 2, pl.ds(done, cells), :],
                preferred_element_type=jnp.float32,
            )
            total = term if total is None else total + term
            done += cells
        total = total.astype(jnp.bfloat16)
        cells = pl.ds(k * BLOCK, BLOCK)
        inner[pl.ds(low, rows), cells] = total[:rows]
        inner[pl.ds(high, rows), cells] = total[rows : 2 * rows]
        outer[pl.ds(low, rows), cells] = total[2 * rows : 3 * rows]
        outer[pl.ds(high, rows), cells] = total[3 * rows :]

    for k in range(n * BLOCKS + 1):
        if k < n * BLOCKS:
            covariances(k)
        if k > 0:
            increments(k - 1)


def update(turn, draws, innov, weights, first_chunk):
    n = len(draws) - 2
    rows, members = innov[0].shape[0] // 4, draws[0].shape[1]
    whole = pl.BlockSpec(memory_space=pltpu.VMEM)
    out = jax.ShapeDtypeStruct((2 * rows, n * CHUNK), jnp.bfloat16)
    window = WINDOW_PATCHES * PC
    return pl.pallas_call(
        functools.partial(update_kernel, n),
        in_specs=[pl.BlockSpec(memory_space=pltpu.SMEM)] + [whole] * (2 * n + 5),
        out_specs=[whole] * 2,
        out_shape=(out, out),
        scratch_shapes=[pltpu.VMEM((2, window, BLOCK), jnp.bfloat16)],
        cost_estimate=pl.CostEstimate(
            flops=2 * n * CHUNK * window * (members + 4 * rows),
            bytes_accessed=2 * (n + 2) * CHUNK * (members + 4 * rows),
            transcendentals=0,
        ),
        compiler_params=pltpu.CompilerParams(vmem_limit_bytes=VMEM_BYTES),
        name="update",
    )(turn, *draws, *innov, weights[first_chunk * BLOCKS : (first_chunk + n) * BLOCKS])


def relay_permutations():
    devices = [
        (x, c, z, y) for x in range(2) for c in range(2) for z in range(4) for y in range(2)
    ]

    def number(x, c, z, y):
        return (x * 2 + c) * 8 + z * 2 + y

    def pairs(move):
        moves = [(device, move(*device)) for device in devices]
        return [(number(*a), number(*b)) for a, b in moves if b is not None]

    def at_home(x, c, y):
        return c == (y ^ (x & 1))

    def segment(x, c, y):
        return 2 * (2 * x + (y ^ (x & 1))) + c

    holders = {segment(x, c, y): (x, c, y) for x in range(2) for c in range(2) for y in range(2)}

    def ring(step):
        def move(x, c, z, y):
            if z not in (1, 2):
                return None
            tx, tc, ty = holders[(segment(x, c, y) + step) % len(holders)]
            return tx, tc, z, ty

        return pairs(move)

    return dict(
        first=pairs(
            lambda x, c, z, y: (x, 1 - c, z, y) if at_home(x, c, y) else (x, c, z, 1 - y)
        ),
        second=pairs(
            lambda x, c, z, y: (x, c, z, y) if at_home(x, c, y) else (x, 1 - c, z, 1 - y)
        ),
        inward=pairs(lambda x, c, z, y: {0: (x, c, 1, y), 3: (x, c, 2, y)}.get(z)),
        outward=pairs(lambda x, c, z, y: {1: (x, c, 0, y), 2: (x, c, 3, y)}.get(z)),
        cross=pairs(lambda x, c, z, y: {1: (x, c, 2, y), 2: (x, c, 1, y)}.get(z)),
        up=ring(1),
        down=ring(-1),
        core=pairs(lambda x, c, z, y: (x, 1 - c, z, y)),
    )


def swapped(pairs):
    return [(target, source) for source, target in pairs]


def relay_shards(bg, jit, inverse_variance, measured, adjacent, tier):
    moves = relay_permutations()

    def send(array, name):
        return lax.ppermute(array, AXES, moves[name])

    def send_back(array, name):
        return lax.ppermute(array, AXES, swapped(moves[name]))

    rows, cells = bg.shape
    members = rows * lax.axis_size("mem")
    half_chunks = cells // 2 // CHUNK
    dom, mem = lax.axis_index("dom"), lax.axis_index("mem")
    x, core, z, y = dom // 2, dom % 2, mem // 2, mem % 2
    home = core == jnp.bitwise_xor(y, x % 2)
    inner = jnp.logical_or(z == 1, z == 2)
    half1 = jnp.where(home, 1 - core, core)
    half2 = 1 - half1
    turn = jnp.where(home, 1 - y, y).astype(jnp.int32).reshape(1)

    gain = gain_of(inverse_variance, measured)[None, :]

    dense = dense_weights(adjacent, tier, members)
    table = lax.all_gather(dense, "mem", axis=0, tiled=True)
    table = jnp.where(home, table, lax.ppermute(table, AXES, moves["core"]))
    half_patches = table.shape[0] // 2
    table = lax.dynamic_slice_in_dim(table, core * half_patches, half_patches, 0)
    table = table.reshape(-1, BLOCK_PATCHES, 2 * REACH + 1)
    spread = [
        jnp.pad(table[:, a, :], ((0, 0), (a, BLOCK_PATCHES - 1 - a))) for a in range(BLOCK_PATCHES)
    ]
    weights = jnp.repeat(jnp.stack(spread, axis=-1), PC, axis=-1)

    last = half_chunks - 1
    arrivals = [[last], [0]] + [[i, i + 1] for i in range(1, last - 2, 2)]
    arrivals += [[i] for i in range(1 + 2 * (len(arrivals) - 2), last)]

    draws, innov = {}, {}
    result = jnp.zeros((rows, cells), jnp.bfloat16)
    todo = list(range(half_chunks))

    for group in arrivals:
        chunks = jnp.array(group, jnp.int32)
        place = jnp.stack([half1 * half_chunks + chunks, half2 * half_chunks + chunks])
        piece1, piece2 = source_pieces(place, bg, jit, gain)
        states, own_innov = collect(send(piece1, "first"), send(piece2, "second"))
        outer_states = send(states, "inward")
        outer_innov = send(own_innov, "inward")
        cross_states = send(states, "cross")
        cross_outer = send(outer_states, "cross")
        for number, chunk in enumerate(group):
            draws[chunk], innov[chunk] = center(
                turn, number, states, own_innov, outer_states, outer_innov, cross_states, cross_outer
            )
        if 0 in draws and last in draws and -1 not in draws:
            draws[-1], innov[-1] = send(draws[last], "up"), send(innov[last], "up")
            draws[last + 1], innov[last + 1] = send(draws[0], "down"), send(innov[0], "down")
        while todo:
            ready = []
            for chunk in todo[: 2 if todo[0] < last - 3 else 1]:
                if all(i in draws for i in (chunk - 1, chunk, chunk + 1)):
                    ready.append(chunk)
            if not ready:
                break
            todo = todo[len(ready) :]
            first = ready[0]
            window = range(first - 1, first + len(ready) + 1)
            inc, inc_outer = update(
                turn, [draws[i] for i in window], [innov[i] for i in window], weights, first
            )
            back = send(inc_outer, "outward")
            inc = jnp.where(inner, inc, back)
            inc1 = send_back(inc[:rows], "first")
            inc2 = send_back(inc[rows:], "second")
            for half, part in ((half1, inc1), (half2, inc2)):
                at = (half * half_chunks + first) * CHUNK
                result = lax.dynamic_update_slice_in_dim(result, part, at, 1)
    return result


def with_halo(block, sides, width):
    for axis, dim in sides:
        count = lax.axis_size(axis)
        forward = [(i, (i + 1) % count) for i in range(count)]
        low = lax.ppermute(
            lax.slice_in_dim(block, block.shape[dim] - width, None, axis=dim), axis, forward
        )
        high = lax.ppermute(
            lax.slice_in_dim(block, 0, width, axis=dim), axis, swapped(forward)
        )
        block = jnp.concatenate([low, block, high], axis=dim)
    return block


def gathered_shards(bg, jit, inverse_variance, measured, adjacent, tier):
    rim_cells = REACH * PC
    gain = gain_of(inverse_variance, measured)
    residual = (
        gain[None, :] * (jit.astype(jnp.float32) - bg.astype(jnp.float32))
    ).astype(jnp.bfloat16)
    states = lax.all_to_all(bg, "mem", split_axis=1, concat_axis=0, tiled=True)
    innov_local = lax.all_to_all(residual, "mem", split_axis=1, concat_axis=0, tiled=True)
    mean = jnp.mean(states.astype(jnp.float32), axis=0)
    draws_local = (states.astype(jnp.float32) - mean[None, :]).astype(jnp.bfloat16)
    padded = with_halo(jnp.stack((draws_local, innov_local)), ((AXES, 2),), rim_cells)
    draws, innov = padded[0], padded[1]
    members = draws.shape[0]
    local_cells = draws.shape[1] - 2 * rim_cells
    local_patches = local_cells // PC
    table = dense_weights(adjacent, tier, members)
    block_size = math.gcd(local_patches, 8)
    window_patches = block_size + 2 * REACH

    def update_block(counter, increment):
        start = counter * block_size
        own = lax.dynamic_slice_in_dim(draws, (REACH + start) * PC, block_size * PC, 1)
        window = lax.dynamic_slice_in_dim(draws, start * PC, window_patches * PC, 1)
        window_innov = lax.dynamic_slice_in_dim(innov, start * PC, window_patches * PC, 1)
        rows = lax.dynamic_slice_in_dim(table, start, block_size, 0)
        weights = jnp.stack(
            [jnp.pad(rows[a], (a, block_size - 1 - a)) for a in range(block_size)]
        )
        covariance = lax.dot_general(
            own, window, (((0,), (0,)), ((), ())), preferred_element_type=jnp.float32
        )
        covariance = covariance.reshape(block_size, PC, window_patches, PC)
        covariance = (covariance * weights[:, None, :, None]).astype(jnp.bfloat16)
        result = lax.dot_general(
            window_innov,
            covariance.reshape(block_size * PC, window_patches * PC),
            (((1,), (1,)), ((), ())),
            preferred_element_type=jnp.float32,
        )
        return lax.dynamic_update_slice_in_dim(
            increment, result.astype(jnp.bfloat16), start * PC, 1
        )

    increment = jnp.zeros((members, local_cells), jnp.bfloat16)
    increment = lax.fori_loop(0, local_patches // block_size, update_block, increment)
    return lax.all_to_all(increment, "mem", split_axis=0, concat_axis=1, tiled=True)


def solution(mesh):
    in_specs = (
        P("mem", "dom"),
        P("mem", "dom"),
        P("dom"),
        P("dom"),
        P(AXES, None),
        P(AXES, None),
    )
    across = mesh.shape["dom"] // 2
    line = mesh.shape["mem"] // across
    shards = relay_shards if (across, line) == (2, 4) else gathered_shards
    return jax.shard_map(
        shards, mesh=mesh, in_specs=in_specs, out_specs=P("mem", "dom"), check_vma=False
    )
```

```python
import functools
import math

import jax
import jax.numpy as jnp
from jax import lax
from jax.experimental import pallas as pl
from jax.experimental.pallas import tpu as pltpu
from jax.sharding import PartitionSpec as P

PC = 64
REACH = 16
NCLASS = 8
AXES = ("dom", "mem")
CHUNK = REACH * PC
BLOCK = 256
BLOCK_PATCHES = BLOCK // PC
BLOCKS = CHUNK // BLOCK
WINDOW_PATCHES = BLOCK_PATCHES + 2 * REACH
VMEM_BYTES = 24 * 2**20
GROUPS = (1, 2, 3, 3, 2, 1)
MOST = 3
SIDE_GROUPS = (1, 1, 1, 3)


def gc_taper(taper_cutoff_length):
    return (
        1.0
        - 5.0 / 3.0 * taper_cutoff_length**2
        + 0.625 * taper_cutoff_length**3
        + 0.5 * taper_cutoff_length**4
        - 0.25 * taper_cutoff_length**5
    )


def gain_of(measurement_inverse_variance, measured_point_number):
    observed = (jnp.arange(PC, dtype=jnp.int32)[None, :] < measured_point_number[:, None]).reshape(
        -1
    )
    return jnp.where(observed, measurement_inverse_variance, jnp.float32(0.0))


def dense_weights(adjacent_region_list, nearby_separation_tier, all_members):
    rows = adjacent_region_list.shape[0]
    groups = lax.axis_size("mem")
    all_patches = rows * lax.axis_size("dom") * groups
    first = (lax.axis_index("dom") * groups + lax.axis_index("mem")) * rows
    own_ids = first + jnp.arange(rows, dtype=jnp.int32)[:, None]
    offset = (
        adjacent_region_list - own_ids + all_patches + all_patches // 2
    ) % all_patches - all_patches // 2
    weight = gc_taper(nearby_separation_tier.astype(jnp.float32) / NCLASS) / (all_members - 1)
    slots = jnp.arange(2 * REACH + 1, dtype=jnp.int32) - REACH
    return jnp.sum(
        jnp.where(offset[:, :, None] == slots[None, None, :], weight[:, :, None], 0.0), axis=1
    )


def whole(array):
    return array, pl.BlockSpec(memory_space=pltpu.VMEM)


def tile(array, number, rows):
    return array, pl.BlockSpec((rows, CHUNK), lambda *_: (number, 0))


def on_one_step(kernel, scalars, inputs, outputs, name, scratch=()):
    inputs, specs = zip(*inputs)
    return pl.pallas_call(
        kernel,
        grid=(1,),
        in_specs=[pl.BlockSpec(memory_space=pltpu.SMEM)] * len(scalars) + list(specs),
        out_specs=[whole(a)[1] for a in outputs],
        out_shape=list(outputs),
        scratch_shapes=list(scratch),
        cost_estimate=pl.CostEstimate(flops=1024, bytes_accessed=1024, transcendentals=0),
        compiler_params=pltpu.CompilerParams(vmem_limit_bytes=VMEM_BYTES),
        name=name,
    )(*scalars, *inputs)


def shape_of(rows, cells):
    return jax.ShapeDtypeStruct((rows, cells), jnp.bfloat16)


def source_rows(bg, jit, gain, piece):
    rows = bg.shape[0]
    piece[pl.ds(0, rows), :] = bg
    piece[pl.ds(rows, rows), :] = (
        gain * (jit.astype(jnp.float32) - bg.astype(jnp.float32))
    ).astype(jnp.bfloat16)


def first_source_kernel(place, bg1, jit1, gain1, bg2, jit2, gain2, piece1, piece2):
    source_rows(bg1[...], jit1[...], gain1[...], piece1)
    source_rows(bg2[...], jit2[...], gain2[...], piece2)


def first_source(place, bg, jit, gain):
    rows, n = bg.shape[0], place.shape[1]

    def specs(piece):
        return [
            pl.BlockSpec((size, CHUNK), lambda i, place: (0, place[piece, i]))
            for size in (rows, rows, 1)
        ]

    out = shape_of(2 * rows * n, CHUNK)
    return pl.pallas_call(
        first_source_kernel,
        grid_spec=pltpu.PrefetchScalarGridSpec(
            num_scalar_prefetch=1,
            grid=(n,),
            in_specs=specs(0) + specs(1),
            out_specs=[pl.BlockSpec((2 * rows, CHUNK), lambda i, place: (i, 0))] * 2,
        ),
        out_shape=(out, out),
        cost_estimate=pl.CostEstimate(flops=1024, bytes_accessed=1024, transcendentals=0),
        name="first_source",
    )(place, bg, jit, gain, bg, jit, gain)


def source_kernel(groups, halves, bg, jit, gain, *pieces):
    half = bg.shape[1] // 2
    rows = 2 * bg.shape[0]
    for side in range(2):
        for group, piece in zip(groups, pieces[side::2]):
            for j, chunk in enumerate(group):
                at = pl.ds(pl.multiple_of(halves[side] * half + chunk * CHUNK, CHUNK), CHUNK)
                source_rows(bg[:, at], jit[:, at], gain[:, at], piece.at[pl.ds(j * rows, rows)])


def source(groups, halves, bg, jit, gain):
    rows = 2 * bg.shape[0]
    outputs = [shape_of(rows * len(group), CHUNK) for group in groups for _ in range(2)]
    inputs = [whole(a) for a in (bg, jit, gain)]
    pieces = on_one_step(
        functools.partial(source_kernel, groups), [halves], inputs, outputs, "source"
    )
    return list(zip(pieces[::2], pieces[1::2]))


def collect_kernel(n, role, *refs):
    own, came, older, (both, across) = refs[:n], refs[n : 2 * n], refs[2 * n : -2], refs[-2:]
    for i in range(n):
        rows = own[i].shape[0] // 2
        for k, part in enumerate((own[i], came[i])):
            both[pl.ds((4 * i + k) * rows, rows), :] = part[pl.ds(0, rows), :]
            both[pl.ds((4 * i + 2 + k) * rows, rows), :] = part[pl.ds(rows, rows), :]
            across[pl.ds((2 * i + k) * rows, rows), :] = part[pl.ds(0, rows), :]
    for i, part in enumerate(older):
        across[pl.ds((n + i) * part.shape[0], part.shape[0]), :] = part[...]


def collect(role, own, came, older):
    n, rows = len(own), own[0][1].block_shape[0]
    outputs = [shape_of(2 * rows * n, CHUNK), shape_of(rows * (n + len(older)), CHUNK)]
    return on_one_step(
        functools.partial(collect_kernel, n), [role], [*own, *came, *older], outputs, "collect"
    )


def center_kernel(role, own, came, outer, outer_innov, across, across_outer, out):
    rows = own.shape[0] // 2
    low = pl.multiple_of(role[0] * rows, rows)
    high = pl.multiple_of((1 - role[0]) * rows, rows)
    own_first = role[0] == 0
    members, lanes = 8 * rows, out.shape[1]

    def in_turn(row, cells):
        mine, other = own[pl.ds(row, rows), cells], came[pl.ds(row, rows), cells]
        return [jnp.where(own_first, mine, other), jnp.where(own_first, other, mine)]

    for j in range(CHUNK // BLOCK):
        cells = pl.ds(j * BLOCK, BLOCK)
        parts = in_turn(0, cells)
        parts += [ref[pl.ds(at, rows), cells] for ref in (outer, across, across_outer) for at in (low, high)]
        parts = [part.astype(jnp.float32) for part in parts]
        total = functools.reduce(jnp.add, parts)
        mean = jnp.sum(total, axis=0, keepdims=True) / members
        perturb = jnp.concatenate([(p - mean).astype(jnp.bfloat16) for p in parts], axis=0)
        out[cells, :] = perturb.T
    for j in range(CHUNK // lanes):
        cells = pl.ds(j * lanes, lanes)
        parts = in_turn(rows, cells) + [outer_innov[pl.ds(at, rows), cells] for at in (low, high)]
        for k, part in enumerate(parts):
            out[pl.ds(CHUNK + (4 * j + k) * rows, rows), :] = part


def centers_kernel(role, *refs):
    n = len(refs) // 7

    @pl.when(role[1] != 0)
    def _():
        for i in range(n):
            center_kernel(role, *refs[6 * i : 6 * i + 6], refs[6 * n + i])


def center(role, chunks):
    rows = chunks[0][0][1].block_shape[0] // 2
    lanes = 8 * rows
    outputs = [shape_of(CHUNK + 4 * rows * (CHUNK // lanes), lanes)] * len(chunks)
    inputs = [part for chunk in chunks for part in chunk]
    return on_one_step(centers_kernel, [role], inputs, outputs, "center")


def window_pieces(b):
    return [(0, b * BLOCK, CHUNK - b * BLOCK), (1, 0, CHUNK), (2, 0, (b + 1) * BLOCK)]


def split_pieces(pieces, lanes):
    for chunk, first, cells in pieces:
        while cells:
            some = min(cells, lanes - first % lanes)
            yield chunk, first, some
            first, cells = first + some, cells - some


def update_kernel(n, first_chunk, role, *refs):
    packed, (weights, inner, outer, covariance) = refs[: n + 2], refs[n + 2 :]
    lanes = packed[0].shape[1]
    rows = lanes // 8
    low, high = role[0] * rows, (1 - role[0]) * rows

    patch = lax.broadcasted_iota(jnp.int32, (WINDOW_PATCHES, BLOCK), 1) // PC

    def covariances(k):
        i, b = divmod(k, BLOCKS)
        own = packed[i + 1][pl.ds(b * BLOCK, BLOCK), :]
        spread = None
        for a in range(BLOCK_PATCHES):
            column = (first_chunk * BLOCKS + k) * BLOCK_PATCHES + a
            shifted = jnp.concatenate(
                [jnp.zeros((size, 1), jnp.float32) for size in (a,) if size]
                + [weights[:, column : column + 1]]
                + [jnp.zeros((size, 1), jnp.float32) for size in (BLOCK_PATCHES - 1 - a,) if size]
            )
            spread = shifted if spread is None else jnp.where(patch >= a, shifted, spread)
        done = 0
        for chunk, first, cells in window_pieces(b):
            patches = cells // PC
            product = lax.dot_general(
                packed[i + chunk][pl.ds(first, cells), :],
                own,
                (((1,), (1,)), ((), ())),
                preferred_element_type=jnp.float32,
            )
            weight = spread[done : done + patches]
            product = product.reshape(patches, PC, BLOCK) * weight[:, None, :]
            covariance[k % 2, pl.ds(done * PC, cells), :] = product.astype(jnp.bfloat16).reshape(
                cells, BLOCK
            )
            done += patches

    def increments(k):
        i, b = divmod(k, BLOCKS)
        total, done = None, 0
        for chunk, first, cells in split_pieces(window_pieces(b), lanes):
            j, lane = divmod(first, lanes)
            term = jnp.dot(
                packed[i + chunk][pl.ds(CHUNK + 4 * j * rows, 4 * rows), pl.ds(lane, cells)],
                covariance[k % 2, pl.ds(done, cells), :],
                preferred_element_type=jnp.float32,
            )
            total = term if total is None else total + term
            done += cells
        total = total.astype(jnp.bfloat16)
        cells = pl.ds(b * BLOCK, BLOCK)
        for out, at in ((inner, 0), (outer, 2 * rows)):
            for place, first in ((low, at), (high, at + rows)):
                place = pl.multiple_of(2 * i * rows + place, rows)
                out[pl.ds(place, rows), cells] = total[first : first + rows]

    @pl.when(role[1] != 0)
    def _():
        for k in range(n * BLOCKS + 1):
            if k < n * BLOCKS:
                covariances(k)
            if k > 0:
                increments(k - 1)


def update(role, packed, weights, first_chunk):
    n = len(packed) - 2
    members = packed[0].shape[1]
    rows = members // 8
    out = shape_of(2 * rows * n, CHUNK)
    window = WINDOW_PATCHES * PC
    return on_one_step(
        functools.partial(update_kernel, n, first_chunk),
        [role],
        [whole(a) for a in (*packed, weights)],
        [out, out],
        "update",
        scratch=[pltpu.VMEM((2, window, BLOCK), jnp.bfloat16)],
    )


def relay_permutations():
    devices = [
        (x, c, z, y) for x in range(2) for c in range(2) for z in range(4) for y in range(2)
    ]

    def number(x, c, z, y):
        return (x * 2 + c) * 8 + z * 2 + y

    def pairs(move):
        moves = [(device, move(*device)) for device in devices]
        return [(number(*a), number(*b)) for a, b in moves if b is not None]

    def ring(step):
        def move(x, c, z, y):
            if z not in (1, 2):
                return None
            segment = (2 * (2 * x + c) + (y ^ c) + step) % 8
            dom, half = divmod(segment, 2)
            return dom // 2, dom % 2, z, half ^ (dom % 2)

        return pairs(move)

    return dict(
        side=pairs(lambda x, c, z, y: (x, c, z, 1 - y)),
        near=pairs(lambda x, c, z, y: (x, c, z ^ 1, y)),
        inward=pairs(lambda x, c, z, y: {0: (x, c, 1, y), 3: (x, c, 2, y)}.get(z)),
        outward=pairs(lambda x, c, z, y: {1: (x, c, 0, y), 2: (x, c, 3, y)}.get(z)),
        cross=pairs(lambda x, c, z, y: {1: (x, c, 2, y), 2: (x, c, 1, y)}.get(z)),
        up=ring(1),
        down=ring(-1),
    )


def swapped(pairs):
    return [(target, source) for source, target in pairs]


def relay_shards(bg, jit, inverse_variance, measured, adjacent, tier):
    moves = relay_permutations()

    def send(array, name):
        return lax.ppermute(array, AXES, moves[name])

    rows, cells = bg.shape
    members = rows * lax.axis_size("mem")
    half_chunks = cells // 2 // CHUNK
    dom, mem = lax.axis_index("dom"), lax.axis_index("mem")
    core, z, y = dom % 2, mem // 2, mem % 2
    inner = jnp.logical_or(z == 1, z == 2)
    half = jnp.bitwise_xor(y, core)
    halves = jnp.stack([1 - half, half]).astype(jnp.int32)
    role = jnp.stack([y, inner]).astype(jnp.int32)

    def in_order(low_first, mine, other):
        return jnp.concatenate(
            [jnp.where(low_first, mine, other), jnp.where(low_first, other, mine)], axis=0
        )

    def after(value, *others):
        return lax.optimization_barrier((value, others))[0]

    gain = gain_of(inverse_variance, measured)[None, :]
    last = half_chunks - 1
    order = [last, *range(last)]
    groups = []
    for size in GROUPS:
        groups.append(order[:size])
        order = order[size:]
    assert not order and all(groups)
    count = len(groups)
    sides, home = [], []
    for size in SIDE_GROUPS:
        taken = groups[len(home) : len(home) + size]
        first = 0
        for group in taken:
            home.append((len(sides), first))
            first += len(group)
        sides.append([chunk for group in taken for chunk in group])

    first_chunks = jnp.array(sides[0], jnp.int32)
    away, own = first_source(
        halves[:, None] * half_chunks + first_chunks[None, :], bg, jit, gain
    )
    came = [send(away, "side")]
    owns = [own]
    pieces = source(sides[1:], after(halves, away), bg, jit, gain)
    token = after(role, pieces[0][0])
    came.append(send(after(pieces[0][0], away), "side"))
    owns += [piece[1] for piece in pieces]
    table = after(dense_weights(adjacent, tier, members), token)

    packed = {}
    result = jnp.zeros((rows, cells), jnp.bfloat16)
    todo = list(range(half_chunks))
    outer, across = [], []
    worked, going_out, going_back = [], [], []

    def parts(t):
        number, first = home[t]
        places = [first + i for i in range(len(groups[t]))]
        return [[tile(array[number], k, 2 * rows) for k in places] for array in (owns, came)]

    def outer_states(t):
        return [tile(outer[t], 2 * i, 2 * rows) for i in range(len(groups[t]))]

    def take_back():
        nonlocal result, token
        for chunks, mine, other in going_back:
            for i, chunk in enumerate(chunks):
                for side, part in ((half, mine), (1 - half, other)):
                    at = (side * half_chunks + chunk) * CHUNK
                    result = lax.dynamic_update_slice_in_dim(result, part[i], at, 1)
        if going_back:
            result, token = lax.optimization_barrier((result, token))
        going_back.clear()

    def send_on(items):
        nonlocal token
        for chunks, inc, back in items:
            inc = jnp.where(inner, inc, after(back, token)).reshape(len(chunks), 2, rows, CHUNK)
            other = inc[:, 1].reshape(-1, CHUNK)
            token = after(token, other)
            other = send(other, "side").reshape(-1, rows, CHUNK)
            going_back.append((chunks, inc[:, 0], other))

    def work(t):
        nonlocal token
        mine, others = parts(t)
        ahead = len(groups[t + 1]) if t + 1 < count else 0
        chunks = center(
            token,
            [
                [mine[i], others[i]]
                + [tile(outer[t], 2 * i, 2 * rows), tile(outer[t], 2 * i + 1, 2 * rows)]
                + [tile(across[t], i, 2 * rows), tile(across[t + 1], ahead + i, 2 * rows)]
                for i in range(len(mine))
            ],
        )
        packed.update(zip(groups[t], chunks))
        token = after(role, chunks[0])
        ready = [i for i in todo if all(j in packed for j in (i - 1, i, i + 1))]
        while ready:
            n = 1
            while n < MOST and t < count - 2 and ready[0] + n in ready:
                n += 1
            now, ready = ready[:n], ready[n:]
            window = [packed[i] for i in range(now[0] - 1, now[-1] + 2)]
            inc, inc_outer = update(token, window, weights, now[0])
            for i in now:
                todo.remove(i)
            token = after(role, inc)
            worked.append((now, inc, inc_outer))
            if t >= count - 2:
                send_out()

    def send_out():
        for now, inc, inc_outer in worked:
            going_out.append((now, inc, send(after(inc_outer, token), "outward")))
        worked.clear()

    for t in range(count + 1):
        if t == 0:
            side_table = send(table, "side")
        if t == 1:
            token = after(token, side_table)
            table = in_order(y == 0, table, side_table)
            near_table = send(table, "near")
        if t == 2:
            token = after(token, near_table)
            table = in_order(z % 2 == 0, table, near_table)
            far_table = send(table, "cross")
        if t == 3:
            token = after(token, far_table)
            weights = jnp.transpose(jnp.where(half == z // 2, table, far_table))
        if t > 0:
            token = after(token, outer[t - 1], across[t - 1])
        if t == 4:
            token = after(token, packed[-1])
        if t == 5:
            token = after(token, packed[last + 1])
        send_out()
        if t < count:
            states, cross = collect(token, *parts(t), outer_states(t - 1) if t else [])
            outer.append(send(states, "inward"))
            if t + 1 < len(SIDE_GROUPS) and t + 1 >= len(came):
                came.append(send(after(pieces[t][0], cross), "side"))
        else:
            older = outer[t - 1].reshape(-1, 2, 2 * rows, CHUNK)
            cross = older[:, 0].reshape(-1, CHUNK)
        token = after(role, cross)
        across.append(send(cross, "cross"))
        take_back()
        ending = len(going_out)
        if t >= 2:
            work(t - 2)
        send_on(going_out[:ending])
        del going_out[:ending]
        if t == 2:
            packed[-1] = send(after(packed[last], token), "up")
        if t == 3:
            packed[last + 1] = send(after(packed[0], token), "down")
    token = after(token, across[count])
    work(count - 1)
    send_on(going_out)
    take_back()
    return result


def with_halo(block, sides, width):
    for axis, dim in sides:
        count = lax.axis_size(axis)
        forward = [(i, (i + 1) % count) for i in range(count)]
        low = lax.ppermute(
            lax.slice_in_dim(block, block.shape[dim] - width, None, axis=dim), axis, forward
        )
        high = lax.ppermute(
            lax.slice_in_dim(block, 0, width, axis=dim), axis, swapped(forward)
        )
        block = jnp.concatenate([low, block, high], axis=dim)
    return block


def gathered_shards(bg, jit, inverse_variance, measured, adjacent, tier):
    rim_cells = REACH * PC
    gain = gain_of(inverse_variance, measured)
    residual = (
        gain[None, :] * (jit.astype(jnp.float32) - bg.astype(jnp.float32))
    ).astype(jnp.bfloat16)
    states = lax.all_to_all(bg, "mem", split_axis=1, concat_axis=0, tiled=True)
    innov_local = lax.all_to_all(residual, "mem", split_axis=1, concat_axis=0, tiled=True)
    mean = jnp.mean(states.astype(jnp.float32), axis=0)
    draws_local = (states.astype(jnp.float32) - mean[None, :]).astype(jnp.bfloat16)
    padded = with_halo(jnp.stack((draws_local, innov_local)), ((AXES, 2),), rim_cells)
    draws, innov = padded[0], padded[1]
    members = draws.shape[0]
    local_cells = draws.shape[1] - 2 * rim_cells
    local_patches = local_cells // PC
    table = dense_weights(adjacent, tier, members)
    block_size = math.gcd(local_patches, 8)
    window_patches = block_size + 2 * REACH

    def update_block(counter, increment):
        start = counter * block_size
        own = lax.dynamic_slice_in_dim(draws, (REACH + start) * PC, block_size * PC, 1)
        window = lax.dynamic_slice_in_dim(draws, start * PC, window_patches * PC, 1)
        window_innov = lax.dynamic_slice_in_dim(innov, start * PC, window_patches * PC, 1)
        rows = lax.dynamic_slice_in_dim(table, start, block_size, 0)
        weights = jnp.stack(
            [jnp.pad(rows[a], (a, block_size - 1 - a)) for a in range(block_size)]
        )
        covariance = lax.dot_general(
            own, window, (((0,), (0,)), ((), ())), preferred_element_type=jnp.float32
        )
        covariance = covariance.reshape(block_size, PC, window_patches, PC)
        covariance = (covariance * weights[:, None, :, None]).astype(jnp.bfloat16)
        result = lax.dot_general(
            window_innov,
            covariance.reshape(block_size * PC, window_patches * PC),
            (((1,), (1,)), ((), ())),
            preferred_element_type=jnp.float32,
        )
        return lax.dynamic_update_slice_in_dim(
            increment, result.astype(jnp.bfloat16), start * PC, 1
        )

    increment = jnp.zeros((members, local_cells), jnp.bfloat16)
    increment = lax.fori_loop(0, local_patches // block_size, update_block, increment)
    return lax.all_to_all(increment, "mem", split_axis=0, concat_axis=1, tiled=True)


def solution(mesh):
    in_specs = (
        P("mem", "dom"),
        P("mem", "dom"),
        P("dom"),
        P("dom"),
        P(AXES, None),
        P(AXES, None),
    )
    across = mesh.shape["dom"] // 2
    line = mesh.shape["mem"] // across
    shards = relay_shards if (across, line) == (2, 4) else gathered_shards
    return jax.shard_map(
        shards, mesh=mesh, in_specs=in_specs, out_specs=P("mem", "dom"), check_vma=False
    )
```

```python
import functools
import math

import jax
import jax.numpy as jnp
from jax import lax
from jax.experimental import pallas as pl
from jax.experimental.pallas import tpu as pltpu
from jax.sharding import PartitionSpec as P

PC = 64
REACH = 16
NCLASS = 8
AXES = ("dom", "mem")
CHUNK = REACH * PC
BLOCK = 256
BLOCK_PATCHES = BLOCK // PC
BLOCKS = CHUNK // BLOCK
WINDOW_PATCHES = BLOCK_PATCHES + 2 * REACH
VMEM_BYTES = 24 * 2**20
GROUPS = (1, 2, 3, 3, 2, 1)
MOST = 3
SIDE_GROUPS = (1, 1, 1, 3)


def gc_taper(taper_cutoff_length):
    return (
        1.0
        - 5.0 / 3.0 * taper_cutoff_length**2
        + 0.625 * taper_cutoff_length**3
        + 0.5 * taper_cutoff_length**4
        - 0.25 * taper_cutoff_length**5
    )


def gain_of(measurement_inverse_variance, measured_point_number):
    observed = (jnp.arange(PC, dtype=jnp.int32)[None, :] < measured_point_number[:, None]).reshape(
        -1
    )
    return jnp.where(observed, measurement_inverse_variance, jnp.float32(0.0))


def dense_weights(adjacent_region_list, nearby_separation_tier, all_members):
    rows = adjacent_region_list.shape[0]
    groups = lax.axis_size("mem")
    all_patches = rows * lax.axis_size("dom") * groups
    first = (lax.axis_index("dom") * groups + lax.axis_index("mem")) * rows
    own_ids = first + jnp.arange(rows, dtype=jnp.int32)[:, None]
    offset = (
        adjacent_region_list - own_ids + all_patches + all_patches // 2
    ) % all_patches - all_patches // 2
    weight = gc_taper(nearby_separation_tier.astype(jnp.float32) / NCLASS) / (all_members - 1)
    slots = jnp.arange(2 * REACH + 1, dtype=jnp.int32) - REACH
    return jnp.sum(
        jnp.where(offset[:, :, None] == slots[None, None, :], weight[:, :, None], 0.0), axis=1
    )


def whole(array):
    return array, pl.BlockSpec(memory_space=pltpu.VMEM)


def tile(array, number, rows):
    return array, pl.BlockSpec((rows, CHUNK), lambda *_: (number, 0))


def on_one_step(kernel, scalars, inputs, outputs, name, scratch=()):
    inputs, specs = zip(*inputs)
    return pl.pallas_call(
        kernel,
        grid=(1,),
        in_specs=[pl.BlockSpec(memory_space=pltpu.SMEM)] * len(scalars) + list(specs),
        out_specs=[whole(a)[1] for a in outputs],
        out_shape=list(outputs),
        scratch_shapes=list(scratch),
        cost_estimate=pl.CostEstimate(flops=1024, bytes_accessed=1024, transcendentals=0),
        compiler_params=pltpu.CompilerParams(vmem_limit_bytes=VMEM_BYTES),
        name=name,
    )(*scalars, *inputs)


def shape_of(rows, cells):
    return jax.ShapeDtypeStruct((rows, cells), jnp.bfloat16)


def source_rows(bg, jit, gain, piece):
    rows = bg.shape[0]
    piece[pl.ds(0, rows), :] = bg
    piece[pl.ds(rows, rows), :] = (
        gain * (jit.astype(jnp.float32) - bg.astype(jnp.float32))
    ).astype(jnp.bfloat16)


def gain_row(inverse_variance, measured, first):
    cell = lax.broadcasted_iota(jnp.int32, (1, CHUNK), 1)
    number = jnp.zeros((1, CHUNK), jnp.int32)
    for patch in range(CHUNK // PC):
        number = jnp.where(cell // PC == patch, measured[first + patch], number)
    return jnp.where(cell % PC < number, inverse_variance, 0.0)


def first_source_kernel(place, measured, bg1, jit1, var1, bg2, jit2, var2, piece1, piece2):
    for piece, bg, jit, var, out in ((0, bg1, jit1, var1, piece1), (1, bg2, jit2, var2, piece2)):
        first = place[piece, pl.program_id(0)] * (CHUNK // PC)
        source_rows(bg[...], jit[...], gain_row(var[...], measured, first), out)


def first_source(place, measured, bg, jit, inverse_variance):
    rows, n = bg.shape[0], place.shape[1]

    def specs(piece):
        return [
            pl.BlockSpec((size, CHUNK), lambda i, place, _: (0, place[piece, i]))
            for size in (rows, rows, 1)
        ]

    out = shape_of(2 * rows * n, CHUNK)
    return pl.pallas_call(
        first_source_kernel,
        grid_spec=pltpu.PrefetchScalarGridSpec(
            num_scalar_prefetch=2,
            grid=(n,),
            in_specs=specs(0) + specs(1),
            out_specs=[pl.BlockSpec((2 * rows, CHUNK), lambda i, place, _: (i, 0))] * 2,
        ),
        out_shape=(out, out),
        cost_estimate=pl.CostEstimate(flops=1024, bytes_accessed=1024, transcendentals=0),
        name="first_source",
    )(place, measured, bg, jit, inverse_variance, bg, jit, inverse_variance)


def source_kernel(groups, halves, bg, jit, gain, *pieces):
    half = bg.shape[1] // 2
    rows = 2 * bg.shape[0]
    for side in range(2):
        for group, piece in zip(groups, pieces[side::2]):
            for j, chunk in enumerate(group):
                at = pl.ds(pl.multiple_of(halves[side] * half + chunk * CHUNK, CHUNK), CHUNK)
                source_rows(bg[:, at], jit[:, at], gain[:, at], piece.at[pl.ds(j * rows, rows)])


def source(groups, halves, bg, jit, gain):
    rows = 2 * bg.shape[0]
    outputs = [shape_of(rows * len(group), CHUNK) for group in groups for _ in range(2)]
    inputs = [whole(a) for a in (bg, jit, gain)]
    pieces = on_one_step(
        functools.partial(source_kernel, groups), [halves], inputs, outputs, "source"
    )
    return list(zip(pieces[::2], pieces[1::2]))


def collect_kernel(n, role, *refs):
    own, came, older, (both, across) = refs[:n], refs[n : 2 * n], refs[2 * n : -2], refs[-2:]
    for i in range(n):
        rows = own[i].shape[0] // 2
        for k, part in enumerate((own[i], came[i])):
            both[pl.ds((4 * i + k) * rows, rows), :] = part[pl.ds(0, rows), :]
            both[pl.ds((4 * i + 2 + k) * rows, rows), :] = part[pl.ds(rows, rows), :]
            across[pl.ds((2 * i + k) * rows, rows), :] = part[pl.ds(0, rows), :]
    for i, part in enumerate(older):
        across[pl.ds((n + i) * part.shape[0], part.shape[0]), :] = part[...]


def collect(role, own, came, older):
    n, rows = len(own), own[0][1].block_shape[0]
    outputs = [shape_of(2 * rows * n, CHUNK), shape_of(rows * (n + len(older)), CHUNK)]
    return on_one_step(
        functools.partial(collect_kernel, n), [role], [*own, *came, *older], outputs, "collect"
    )


def center_kernel(role, own, came, outer, outer_innov, across, across_outer, out):
    rows = own.shape[0] // 2
    low = pl.multiple_of(role[0] * rows, rows)
    high = pl.multiple_of((1 - role[0]) * rows, rows)
    own_first = role[0] == 0
    members, lanes = 8 * rows, out.shape[1]

    def in_turn(row, cells):
        mine, other = own[pl.ds(row, rows), cells], came[pl.ds(row, rows), cells]
        return [jnp.where(own_first, mine, other), jnp.where(own_first, other, mine)]

    for j in range(CHUNK // BLOCK):
        cells = pl.ds(j * BLOCK, BLOCK)
        parts = in_turn(0, cells)
        parts += [ref[pl.ds(at, rows), cells] for ref in (outer, across, across_outer) for at in (low, high)]
        parts = [part.astype(jnp.float32) for part in parts]
        total = functools.reduce(jnp.add, parts)
        mean = jnp.sum(total, axis=0, keepdims=True) / members
        perturb = jnp.concatenate([(p - mean).astype(jnp.bfloat16) for p in parts], axis=0)
        out[cells, :] = perturb.T
    for j in range(CHUNK // lanes):
        cells = pl.ds(j * lanes, lanes)
        parts = in_turn(rows, cells) + [outer_innov[pl.ds(at, rows), cells] for at in (low, high)]
        for k, part in enumerate(parts):
            out[pl.ds(CHUNK + (4 * j + k) * rows, rows), :] = part


def centers_kernel(role, *refs):
    n = len(refs) // 7

    @pl.when(role[1] != 0)
    def _():
        for i in range(n):
            center_kernel(role, *refs[6 * i : 6 * i + 6], refs[6 * n + i])


def center(role, chunks):
    rows = chunks[0][0][1].block_shape[0] // 2
    lanes = 8 * rows
    outputs = [shape_of(CHUNK + 4 * rows * (CHUNK // lanes), lanes)] * len(chunks)
    inputs = [part for chunk in chunks for part in chunk]
    return on_one_step(centers_kernel, [role], inputs, outputs, "center")


def window_pieces(b):
    return [(0, b * BLOCK, CHUNK - b * BLOCK), (1, 0, CHUNK), (2, 0, (b + 1) * BLOCK)]


def split_pieces(pieces, lanes):
    for chunk, first, cells in pieces:
        while cells:
            some = min(cells, lanes - first % lanes)
            yield chunk, first, some
            first, cells = first + some, cells - some


def update_kernel(n, first_chunk, role, *refs):
    packed, (weights, inner, outer, covariance) = refs[: n + 2], refs[n + 2 :]
    lanes = packed[0].shape[1]
    rows = lanes // 8
    low, high = role[0] * rows, (1 - role[0]) * rows

    patch = lax.broadcasted_iota(jnp.int32, (WINDOW_PATCHES, BLOCK), 1) // PC

    def covariances(k):
        i, b = divmod(k, BLOCKS)
        own = packed[i + 1][pl.ds(b * BLOCK, BLOCK), :]
        spread = None
        for a in range(BLOCK_PATCHES):
            column = (first_chunk * BLOCKS + k) * BLOCK_PATCHES + a
            shifted = jnp.concatenate(
                [jnp.zeros((size, 1), jnp.float32) for size in (a,) if size]
                + [weights[:, column : column + 1]]
                + [jnp.zeros((size, 1), jnp.float32) for size in (BLOCK_PATCHES - 1 - a,) if size]
            )
            spread = shifted if spread is None else jnp.where(patch >= a, shifted, spread)
        done = 0
        for chunk, first, cells in window_pieces(b):
            patches = cells // PC
            product = lax.dot_general(
                packed[i + chunk][pl.ds(first, cells), :],
                own,
                (((1,), (1,)), ((), ())),
                preferred_element_type=jnp.float32,
            )
            weight = spread[done : done + patches]
            product = product.reshape(patches, PC, BLOCK) * weight[:, None, :]
            covariance[k % 2, pl.ds(done * PC, cells), :] = product.astype(jnp.bfloat16).reshape(
                cells, BLOCK
            )
            done += patches

    def increments(k):
        i, b = divmod(k, BLOCKS)
        total, done = None, 0
        for chunk, first, cells in split_pieces(window_pieces(b), lanes):
            j, lane = divmod(first, lanes)
            term = jnp.dot(
                packed[i + chunk][pl.ds(CHUNK + 4 * j * rows, 4 * rows), pl.ds(lane, cells)],
                covariance[k % 2, pl.ds(done, cells), :],
                preferred_element_type=jnp.float32,
            )
            total = term if total is None else total + term
            done += cells
        total = total.astype(jnp.bfloat16)
        cells = pl.ds(b * BLOCK, BLOCK)
        for out, at in ((inner, 0), (outer, 2 * rows)):
            for place, first in ((low, at), (high, at + rows)):
                place = pl.multiple_of(2 * i * rows + place, rows)
                out[pl.ds(place, rows), cells] = total[first : first + rows]

    @pl.when(role[1] != 0)
    def _():
        for k in range(n * BLOCKS + 1):
            if k < n * BLOCKS:
                covariances(k)
            if k > 0:
                increments(k - 1)


def update(role, packed, weights, first_chunk):
    n = len(packed) - 2
    members = packed[0].shape[1]
    rows = members // 8
    out = shape_of(2 * rows * n, CHUNK)
    window = WINDOW_PATCHES * PC
    return on_one_step(
        functools.partial(update_kernel, n, first_chunk),
        [role],
        [whole(a) for a in (*packed, weights)],
        [out, out],
        "update",
        scratch=[pltpu.VMEM((2, window, BLOCK), jnp.bfloat16)],
    )


def assemble_kernel(groups, half_chunks, role, *refs):
    out = refs[-1]
    rows = out.shape[0]

    def cells(half, chunk):
        first = half * (half_chunks * CHUNK) + chunk * CHUNK
        return pl.ds(pl.multiple_of(first, CHUNK), CHUNK)

    for k, group in enumerate(groups):
        inc, back, other = refs[3 * k : 3 * k + 3]
        for i, chunk in enumerate(group):
            out[:, cells(1 - role[2], chunk)] = other[pl.ds(i * rows, rows), :]
            for inner, mine in ((1, inc), (0, back)):

                @pl.when(role[1] == inner)
                def _():
                    out[:, cells(role[2], chunk)] = mine[pl.ds(2 * i * rows, rows), :]


def assemble(role, finished, half_chunks):
    groups = [tuple(chunks) for chunks, *_ in finished]
    inputs = [whole(part) for _, *parts in finished for part in parts]
    rows = finished[0][3].shape[0] // len(groups[0])
    out = shape_of(rows, 2 * half_chunks * CHUNK)
    return pl.pallas_call(
        functools.partial(assemble_kernel, groups, half_chunks),
        grid=(1,),
        in_specs=[pl.BlockSpec(memory_space=pltpu.SMEM)] + [spec for _, spec in inputs],
        out_specs=pl.BlockSpec(out.shape, lambda *_: (0, 0)),
        out_shape=out,
        cost_estimate=pl.CostEstimate(flops=1024, bytes_accessed=1024, transcendentals=0),
        compiler_params=pltpu.CompilerParams(vmem_limit_bytes=VMEM_BYTES),
        name="assemble",
    )(role, *[array for array, _ in inputs])


def relay_permutations():
    devices = [
        (x, c, z, y) for x in range(2) for c in range(2) for z in range(4) for y in range(2)
    ]

    def number(x, c, z, y):
        return (x * 2 + c) * 8 + z * 2 + y

    def pairs(move):
        moves = [(device, move(*device)) for device in devices]
        return [(number(*a), number(*b)) for a, b in moves if b is not None]

    def ring(step):
        def move(x, c, z, y):
            if z not in (1, 2):
                return None
            segment = (2 * (2 * x + c) + (y ^ c) + step) % 8
            dom, half = divmod(segment, 2)
            return dom // 2, dom % 2, z, half ^ (dom % 2)

        return pairs(move)

    return dict(
        side=pairs(lambda x, c, z, y: (x, c, z, 1 - y)),
        near=pairs(lambda x, c, z, y: (x, c, z ^ 1, y)),
        inward=pairs(lambda x, c, z, y: {0: (x, c, 1, y), 3: (x, c, 2, y)}.get(z)),
        outward=pairs(lambda x, c, z, y: {1: (x, c, 0, y), 2: (x, c, 3, y)}.get(z)),
        cross=pairs(lambda x, c, z, y: {1: (x, c, 2, y), 2: (x, c, 1, y)}.get(z)),
        up=ring(1),
        down=ring(-1),
    )


def swapped(pairs):
    return [(target, source) for source, target in pairs]


def relay_shards(bg, jit, inverse_variance, measured, adjacent, tier):
    moves = relay_permutations()

    def send(array, name):
        return lax.ppermute(array, AXES, moves[name])

    rows, cells = bg.shape
    members = rows * lax.axis_size("mem")
    half_chunks = cells // 2 // CHUNK
    dom, mem = lax.axis_index("dom"), lax.axis_index("mem")
    core, z, y = dom % 2, mem // 2, mem % 2
    inner = jnp.logical_or(z == 1, z == 2)
    half = jnp.bitwise_xor(y, core)
    halves = jnp.stack([1 - half, half]).astype(jnp.int32)
    role = jnp.stack([y, inner]).astype(jnp.int32)

    def in_order(low_first, mine, other):
        return jnp.concatenate(
            [jnp.where(low_first, mine, other), jnp.where(low_first, other, mine)], axis=0
        )

    def after(value, *others):
        return lax.optimization_barrier((value, others))[0]

    gain = gain_of(inverse_variance, measured)[None, :]
    last = half_chunks - 1
    order = [last, *range(last)]
    groups = []
    for size in GROUPS:
        groups.append(order[:size])
        order = order[size:]
    assert not order and all(groups)
    count = len(groups)
    sides, home = [], []
    for size in SIDE_GROUPS:
        taken = groups[len(home) : len(home) + size]
        first = 0
        for group in taken:
            home.append((len(sides), first))
            first += len(group)
        sides.append([chunk for group in taken for chunk in group])

    first_chunks = jnp.array(sides[0], jnp.int32)
    away, own = first_source(
        halves[:, None] * half_chunks + first_chunks[None, :],
        measured,
        bg,
        jit,
        inverse_variance[None, :],
    )
    came = [send(away, "side")]
    owns = [own]
    pieces = source(sides[1:], after(halves, away), bg, jit, gain)
    token = after(role, pieces[0][0])
    came.append(send(after(pieces[0][0], away), "side"))
    owns += [piece[1] for piece in pieces]
    table = after(dense_weights(adjacent, tier, members), token)

    packed = {}
    finished = []
    todo = list(range(half_chunks))
    outer, across = [], []
    worked, going_out, going_back = [], [], []

    def parts(t):
        number, first = home[t]
        places = [first + i for i in range(len(groups[t]))]
        return [[tile(array[number], k, 2 * rows) for k in places] for array in (owns, came)]

    def outer_states(t):
        return [tile(outer[t], 2 * i, 2 * rows) for i in range(len(groups[t]))]

    def take_back():
        nonlocal token
        for chunks, inc, back, other in going_back:
            token = after(token, other)
            finished.append((chunks, inc, back, other))
        going_back.clear()

    def send_on(items):
        nonlocal token
        for chunks, inc, back in items:
            back = after(back, token)
            pairs = [part.reshape(len(chunks), 2, rows, CHUNK)[:, 1] for part in (inc, back)]
            other = jnp.where(inner, *pairs).reshape(-1, CHUNK)
            token = after(token, other)
            going_back.append((chunks, inc, back, send(other, "side")))

    def work(t):
        nonlocal token
        mine, others = parts(t)
        ahead = len(groups[t + 1]) if t + 1 < count else 0
        chunks = center(
            token,
            [
                [mine[i], others[i]]
                + [tile(outer[t], 2 * i, 2 * rows), tile(outer[t], 2 * i + 1, 2 * rows)]
                + [tile(across[t], i, 2 * rows), tile(across[t + 1], ahead + i, 2 * rows)]
                for i in range(len(mine))
            ],
        )
        packed.update(zip(groups[t], chunks))
        token = after(role, chunks[0])
        ready = [i for i in todo if all(j in packed for j in (i - 1, i, i + 1))]
        while ready:
            n = 1
            while n < MOST and t < count - 2 and ready[0] + n in ready:
                n += 1
            now, ready = ready[:n], ready[n:]
            if t == count - 1 and len(going_out) > 2:
                token = after(token, going_out[-3][2])
            window = [packed[i] for i in range(now[0] - 1, now[-1] + 2)]
            inc, inc_outer = update(token, window, weights, now[0])
            for i in now:
                todo.remove(i)
            token = after(role, inc)
            worked.append((now, inc, inc_outer))
            if t >= count - 2:
                send_out()

    def send_out():
        for now, inc, inc_outer in worked:
            going_out.append((now, inc, send(after(inc_outer, token), "outward")))
        worked.clear()

    for t in range(count + 1):
        if t == 0:
            side_table = send(table, "side")
        if t == 1:
            token = after(token, side_table)
            table = in_order(y == 0, table, side_table)
            near_table = send(table, "near")
        if t == 2:
            token = after(token, near_table)
            table = in_order(z % 2 == 0, table, near_table)
            far_table = send(table, "cross")
        if t == 3:
            token = after(token, far_table)
            weights = jnp.transpose(jnp.where(half == z // 2, table, far_table))
        if t > 0:
            token = after(token, outer[t - 1], across[t - 1])
        if t == 4:
            token = after(token, packed[-1])
        if t == 5:
            token = after(token, packed[last + 1])
        if t < count:
            states, cross = collect(token, *parts(t), outer_states(t - 1) if t else [])
            outer.append(send(states, "inward"))
            if t + 1 < len(SIDE_GROUPS) and t + 1 >= len(came):
                came.append(send(after(pieces[t][0], cross), "side"))
        else:
            older = outer[t - 1].reshape(-1, 2, 2 * rows, CHUNK)
            cross = older[:, 0].reshape(-1, CHUNK)
        token = after(role, cross)
        across.append(send(cross, "cross"))
        send_out()
        take_back()
        ending = len(going_out)
        if t >= 2:
            work(t - 2)
        send_on(going_out[:ending])
        del going_out[:ending]
        if t == 2:
            packed[-1] = send(after(packed[last], token), "up")
        if t == 3:
            packed[last + 1] = send(after(packed[0], token), "down")
    token = after(token, across[count])
    work(count - 1)
    send_on(going_out)
    take_back()
    return assemble(jnp.append(role, half), finished, half_chunks)


def with_halo(block, sides, width):
    for axis, dim in sides:
        count = lax.axis_size(axis)
        forward = [(i, (i + 1) % count) for i in range(count)]
        low = lax.ppermute(
            lax.slice_in_dim(block, block.shape[dim] - width, None, axis=dim), axis, forward
        )
        high = lax.ppermute(
            lax.slice_in_dim(block, 0, width, axis=dim), axis, swapped(forward)
        )
        block = jnp.concatenate([low, block, high], axis=dim)
    return block


def gathered_shards(bg, jit, inverse_variance, measured, adjacent, tier):
    rim_cells = REACH * PC
    gain = gain_of(inverse_variance, measured)
    residual = (
        gain[None, :] * (jit.astype(jnp.float32) - bg.astype(jnp.float32))
    ).astype(jnp.bfloat16)
    states = lax.all_to_all(bg, "mem", split_axis=1, concat_axis=0, tiled=True)
    innov_local = lax.all_to_all(residual, "mem", split_axis=1, concat_axis=0, tiled=True)
    mean = jnp.mean(states.astype(jnp.float32), axis=0)
    draws_local = (states.astype(jnp.float32) - mean[None, :]).astype(jnp.bfloat16)
    padded = with_halo(jnp.stack((draws_local, innov_local)), ((AXES, 2),), rim_cells)
    draws, innov = padded[0], padded[1]
    members = draws.shape[0]
    local_cells = draws.shape[1] - 2 * rim_cells
    local_patches = local_cells // PC
    table = dense_weights(adjacent, tier, members)
    block_size = math.gcd(local_patches, 8)
    window_patches = block_size + 2 * REACH

    def update_block(counter, increment):
        start = counter * block_size
        own = lax.dynamic_slice_in_dim(draws, (REACH + start) * PC, block_size * PC, 1)
        window = lax.dynamic_slice_in_dim(draws, start * PC, window_patches * PC, 1)
        window_innov = lax.dynamic_slice_in_dim(innov, start * PC, window_patches * PC, 1)
        rows = lax.dynamic_slice_in_dim(table, start, block_size, 0)
        weights = jnp.stack(
            [jnp.pad(rows[a], (a, block_size - 1 - a)) for a in range(block_size)]
        )
        covariance = lax.dot_general(
            own, window, (((0,), (0,)), ((), ())), preferred_element_type=jnp.float32
        )
        covariance = covariance.reshape(block_size, PC, window_patches, PC)
        covariance = (covariance * weights[:, None, :, None]).astype(jnp.bfloat16)
        result = lax.dot_general(
            window_innov,
            covariance.reshape(block_size * PC, window_patches * PC),
            (((1,), (1,)), ((), ())),
            preferred_element_type=jnp.float32,
        )
        return lax.dynamic_update_slice_in_dim(
            increment, result.astype(jnp.bfloat16), start * PC, 1
        )

    increment = jnp.zeros((members, local_cells), jnp.bfloat16)
    increment = lax.fori_loop(0, local_patches // block_size, update_block, increment)
    return lax.all_to_all(increment, "mem", split_axis=0, concat_axis=1, tiled=True)


def solution(mesh):
    in_specs = (
        P("mem", "dom"),
        P("mem", "dom"),
        P("dom"),
        P("dom"),
        P(AXES, None),
        P(AXES, None),
    )
    across = mesh.shape["dom"] // 2
    line = mesh.shape["mem"] // across
    shards = relay_shards if (across, line) == (2, 4) else gathered_shards
    return jax.shard_map(
        shards, mesh=mesh, in_specs=in_specs, out_specs=P("mem", "dom"), check_vma=False
    )
```

```python
import functools
import math

import jax
import jax.numpy as jnp
from jax import lax
from jax.experimental import pallas as pl
from jax.experimental.pallas import tpu as pltpu
from jax.sharding import PartitionSpec as P

PC = 64
REACH = 16
NCLASS = 8
AXES = ("dom", "mem")
CHUNK = REACH * PC
BLOCK = 256
BLOCK_PATCHES = BLOCK // PC
BLOCKS = CHUNK // BLOCK
WINDOW_PATCHES = BLOCK_PATCHES + 2 * REACH
VMEM_BYTES = 24 * 2**20
GROUPS = (1, 2, 3, 2, 2, 1, 1)
MOST = 3
SIDE_GROUPS = (1, 1, 1, 4)


def gc_taper(taper_cutoff_length):
    return (
        1.0
        - 5.0 / 3.0 * taper_cutoff_length**2
        + 0.625 * taper_cutoff_length**3
        + 0.5 * taper_cutoff_length**4
        - 0.25 * taper_cutoff_length**5
    )


def gain_of(measurement_inverse_variance, measured_point_number):
    observed = (jnp.arange(PC, dtype=jnp.int32)[None, :] < measured_point_number[:, None]).reshape(
        -1
    )
    return jnp.where(observed, measurement_inverse_variance, jnp.float32(0.0))


def dense_weights(adjacent_region_list, nearby_separation_tier, all_members):
    rows = adjacent_region_list.shape[0]
    groups = lax.axis_size("mem")
    all_patches = rows * lax.axis_size("dom") * groups
    first = (lax.axis_index("dom") * groups + lax.axis_index("mem")) * rows
    own_ids = first + jnp.arange(rows, dtype=jnp.int32)[:, None]
    offset = (
        adjacent_region_list - own_ids + all_patches + all_patches // 2
    ) % all_patches - all_patches // 2
    weight = gc_taper(nearby_separation_tier.astype(jnp.float32) / NCLASS) / (all_members - 1)
    slots = jnp.arange(2 * REACH + 1, dtype=jnp.int32) - REACH
    return jnp.sum(
        jnp.where(offset[:, :, None] == slots[None, None, :], weight[:, :, None], 0.0), axis=1
    )


def whole(array):
    return array, pl.BlockSpec(memory_space=pltpu.VMEM)


def tile(array, number, rows):
    return array, pl.BlockSpec((rows, CHUNK), lambda *_: (number, 0))


def on_one_step(kernel, scalars, inputs, outputs, name, scratch=()):
    inputs, specs = zip(*inputs)
    return pl.pallas_call(
        kernel,
        grid=(1,),
        in_specs=[pl.BlockSpec(memory_space=pltpu.SMEM)] * len(scalars) + list(specs),
        out_specs=[whole(a)[1] for a in outputs],
        out_shape=list(outputs),
        scratch_shapes=list(scratch),
        cost_estimate=pl.CostEstimate(flops=1024, bytes_accessed=1024, transcendentals=0),
        compiler_params=pltpu.CompilerParams(vmem_limit_bytes=VMEM_BYTES),
        name=name,
    )(*scalars, *inputs)


def shape_of(rows, cells):
    return jax.ShapeDtypeStruct((rows, cells), jnp.bfloat16)


def source_rows(bg, jit, gain, piece):
    rows = bg.shape[0]
    piece[pl.ds(0, rows), :] = bg
    piece[pl.ds(rows, rows), :] = (
        gain * (jit.astype(jnp.float32) - bg.astype(jnp.float32))
    ).astype(jnp.bfloat16)


def gain_row(inverse_variance, measured, first):
    cell = lax.broadcasted_iota(jnp.int32, (1, CHUNK), 1)
    number = jnp.zeros((1, CHUNK), jnp.int32)
    for patch in range(CHUNK // PC):
        number = jnp.where(cell // PC == patch, measured[first + patch], number)
    return jnp.where(cell % PC < number, inverse_variance, 0.0)


def first_source_kernel(place, measured, bg1, jit1, var1, bg2, jit2, var2, piece1, piece2):
    for piece, bg, jit, var, out in ((0, bg1, jit1, var1, piece1), (1, bg2, jit2, var2, piece2)):
        first = place[piece, pl.program_id(0)] * (CHUNK // PC)
        source_rows(bg[...], jit[...], gain_row(var[...], measured, first), out)


def first_source(place, measured, bg, jit, inverse_variance):
    rows, n = bg.shape[0], place.shape[1]

    def specs(piece):
        return [
            pl.BlockSpec((size, CHUNK), lambda i, place, _: (0, place[piece, i]))
            for size in (rows, rows, 1)
        ]

    out = shape_of(2 * rows * n, CHUNK)
    return pl.pallas_call(
        first_source_kernel,
        grid_spec=pltpu.PrefetchScalarGridSpec(
            num_scalar_prefetch=2,
            grid=(n,),
            in_specs=specs(0) + specs(1),
            out_specs=[pl.BlockSpec((2 * rows, CHUNK), lambda i, place, _: (i, 0))] * 2,
        ),
        out_shape=(out, out),
        cost_estimate=pl.CostEstimate(flops=1024, bytes_accessed=1024, transcendentals=0),
        name="first_source",
    )(place, measured, bg, jit, inverse_variance, bg, jit, inverse_variance)


def source_kernel(groups, halves, bg, jit, gain, *pieces):
    half = bg.shape[1] // 2
    rows = 2 * bg.shape[0]
    for side in range(2):
        for group, piece in zip(groups, pieces[side::2]):
            for j, chunk in enumerate(group):
                at = pl.ds(pl.multiple_of(halves[side] * half + chunk * CHUNK, CHUNK), CHUNK)
                source_rows(bg[:, at], jit[:, at], gain[:, at], piece.at[pl.ds(j * rows, rows)])


def source(groups, halves, bg, jit, gain):
    rows = 2 * bg.shape[0]
    outputs = [shape_of(rows * len(group), CHUNK) for group in groups for _ in range(2)]
    inputs = [whole(a) for a in (bg, jit, gain)]
    pieces = on_one_step(
        functools.partial(source_kernel, groups), [halves], inputs, outputs, "source"
    )
    return list(zip(pieces[::2], pieces[1::2]))


def collect_kernel(n, role, *refs):
    own, came, older, (both, across) = refs[:n], refs[n : 2 * n], refs[2 * n : -2], refs[-2:]
    for i in range(n):
        rows = own[i].shape[0] // 2
        for k, part in enumerate((own[i], came[i])):
            both[pl.ds((4 * i + k) * rows, rows), :] = part[pl.ds(0, rows), :]
            both[pl.ds((4 * i + 2 + k) * rows, rows), :] = part[pl.ds(rows, rows), :]
            across[pl.ds((2 * i + k) * rows, rows), :] = part[pl.ds(0, rows), :]
    for i, part in enumerate(older):
        across[pl.ds((n + i) * part.shape[0], part.shape[0]), :] = part[...]


def collect(role, own, came, older):
    n, rows = len(own), own[0][1].block_shape[0]
    outputs = [shape_of(2 * rows * n, CHUNK), shape_of(rows * (n + len(older)), CHUNK)]
    return on_one_step(
        functools.partial(collect_kernel, n), [role], [*own, *came, *older], outputs, "collect"
    )


def center_kernel(role, own, came, outer, outer_innov, across, across_outer, out):
    rows = own.shape[0] // 2
    low = pl.multiple_of(role[0] * rows, rows)
    high = pl.multiple_of((1 - role[0]) * rows, rows)
    own_first = role[0] == 0
    members, lanes = 8 * rows, out.shape[1]

    def in_turn(row, cells):
        mine, other = own[pl.ds(row, rows), cells], came[pl.ds(row, rows), cells]
        return [jnp.where(own_first, mine, other), jnp.where(own_first, other, mine)]

    for j in range(CHUNK // BLOCK):
        cells = pl.ds(j * BLOCK, BLOCK)
        parts = in_turn(0, cells)
        parts += [ref[pl.ds(at, rows), cells] for ref in (outer, across, across_outer) for at in (low, high)]
        parts = [part.astype(jnp.float32) for part in parts]
        total = functools.reduce(jnp.add, parts)
        mean = jnp.sum(total, axis=0, keepdims=True) / members
        perturb = jnp.concatenate([(p - mean).astype(jnp.bfloat16) for p in parts], axis=0)
        out[cells, :] = perturb.T
    for j in range(CHUNK // lanes):
        cells = pl.ds(j * lanes, lanes)
        parts = in_turn(rows, cells) + [outer_innov[pl.ds(at, rows), cells] for at in (low, high)]
        for k, part in enumerate(parts):
            out[pl.ds(CHUNK + (4 * j + k) * rows, rows), :] = part


def centers_kernel(role, *refs):
    n = len(refs) // 7

    @pl.when(role[1] != 0)
    def _():
        for i in range(n):
            center_kernel(role, *refs[6 * i : 6 * i + 6], refs[6 * n + i])


def center(role, chunks):
    rows = chunks[0][0][1].block_shape[0] // 2
    lanes = 8 * rows
    outputs = [shape_of(CHUNK + 4 * rows * (CHUNK // lanes), lanes)] * len(chunks)
    inputs = [part for chunk in chunks for part in chunk]
    return on_one_step(centers_kernel, [role], inputs, outputs, "center")


def window_pieces(b):
    return [(0, b * BLOCK, CHUNK - b * BLOCK), (1, 0, CHUNK), (2, 0, (b + 1) * BLOCK)]


def split_pieces(pieces, lanes):
    for chunk, first, cells in pieces:
        while cells:
            some = min(cells, lanes - first % lanes)
            yield chunk, first, some
            first, cells = first + some, cells - some


def update_kernel(n, first_chunk, role, *refs):
    packed, (weights, inner, outer, covariance) = refs[: n + 2], refs[n + 2 :]
    lanes = packed[0].shape[1]
    rows = lanes // 8
    low, high = role[0] * rows, (1 - role[0]) * rows

    patch = lax.broadcasted_iota(jnp.int32, (WINDOW_PATCHES, BLOCK), 1) // PC

    def covariances(k):
        i, b = divmod(k, BLOCKS)
        own = packed[i + 1][pl.ds(b * BLOCK, BLOCK), :]
        spread = None
        for a in range(BLOCK_PATCHES):
            column = (first_chunk * BLOCKS + k) * BLOCK_PATCHES + a
            shifted = jnp.concatenate(
                [jnp.zeros((size, 1), jnp.float32) for size in (a,) if size]
                + [weights[:, column : column + 1]]
                + [jnp.zeros((size, 1), jnp.float32) for size in (BLOCK_PATCHES - 1 - a,) if size]
            )
            spread = shifted if spread is None else jnp.where(patch >= a, shifted, spread)
        done = 0
        for chunk, first, cells in window_pieces(b):
            patches = cells // PC
            product = lax.dot_general(
                packed[i + chunk][pl.ds(first, cells), :],
                own,
                (((1,), (1,)), ((), ())),
                preferred_element_type=jnp.float32,
            )
            weight = spread[done : done + patches]
            product = product.reshape(patches, PC, BLOCK) * weight[:, None, :]
            covariance[k % 2, pl.ds(done * PC, cells), :] = product.astype(jnp.bfloat16).reshape(
                cells, BLOCK
            )
            done += patches

    def increments(k):
        i, b = divmod(k, BLOCKS)
        total, done = None, 0
        for chunk, first, cells in split_pieces(window_pieces(b), lanes):
            j, lane = divmod(first, lanes)
            term = jnp.dot(
                packed[i + chunk][pl.ds(CHUNK + 4 * j * rows, 4 * rows), pl.ds(lane, cells)],
                covariance[k % 2, pl.ds(done, cells), :],
                preferred_element_type=jnp.float32,
            )
            total = term if total is None else total + term
            done += cells
        total = total.astype(jnp.bfloat16)
        cells = pl.ds(b * BLOCK, BLOCK)
        for out, at in ((inner, 0), (outer, 2 * rows)):
            for place, first in ((low, at), (high, at + rows)):
                place = pl.multiple_of(2 * i * rows + place, rows)
                out[pl.ds(place, rows), cells] = total[first : first + rows]

    @pl.when(role[1] != 0)
    def _():
        for k in range(n * BLOCKS + 1):
            if k < n * BLOCKS:
                covariances(k)
            if k > 0:
                increments(k - 1)


def update(role, packed, weights, first_chunk):
    n = len(packed) - 2
    members = packed[0].shape[1]
    rows = members // 8
    out = shape_of(2 * rows * n, CHUNK)
    window = WINDOW_PATCHES * PC
    return on_one_step(
        functools.partial(update_kernel, n, first_chunk),
        [role],
        [whole(a) for a in (*packed, weights)],
        [out, out],
        "update",
        scratch=[pltpu.VMEM((2, window, BLOCK), jnp.bfloat16)],
    )


def assemble_kernel(groups, half_chunks, role, *refs):
    out = refs[-1]
    rows = out.shape[0]

    def cells(half, chunk):
        first = half * (half_chunks * CHUNK) + chunk * CHUNK
        return pl.ds(pl.multiple_of(first, CHUNK), CHUNK)

    for k, group in enumerate(groups):
        inc, back, other = refs[3 * k : 3 * k + 3]
        for i, chunk in enumerate(group):
            out[:, cells(1 - role[2], chunk)] = other[pl.ds(i * rows, rows), :]
            for inner, mine in ((1, inc), (0, back)):

                @pl.when(role[1] == inner)
                def _():
                    out[:, cells(role[2], chunk)] = mine[pl.ds(2 * i * rows, rows), :]


def assemble(role, finished, half_chunks):
    groups = [tuple(chunks) for chunks, *_ in finished]
    inputs = [whole(part) for _, *parts in finished for part in parts]
    rows = finished[0][3].shape[0] // len(groups[0])
    out = shape_of(rows, 2 * half_chunks * CHUNK)
    return pl.pallas_call(
        functools.partial(assemble_kernel, groups, half_chunks),
        grid=(1,),
        in_specs=[pl.BlockSpec(memory_space=pltpu.SMEM)] + [spec for _, spec in inputs],
        out_specs=pl.BlockSpec(out.shape, lambda *_: (0, 0)),
        out_shape=out,
        cost_estimate=pl.CostEstimate(flops=1024, bytes_accessed=1024, transcendentals=0),
        compiler_params=pltpu.CompilerParams(vmem_limit_bytes=VMEM_BYTES),
        name="assemble",
    )(role, *[array for array, _ in inputs])


def relay_permutations():
    devices = [
        (x, c, z, y) for x in range(2) for c in range(2) for z in range(4) for y in range(2)
    ]

    def number(x, c, z, y):
        return (x * 2 + c) * 8 + z * 2 + y

    def pairs(move):
        moves = [(device, move(*device)) for device in devices]
        return [(number(*a), number(*b)) for a, b in moves if b is not None]

    def ring(step):
        def move(x, c, z, y):
            if z not in (1, 2):
                return None
            segment = (2 * (2 * x + c) + (y ^ c) + step) % 8
            dom, half = divmod(segment, 2)
            return dom // 2, dom % 2, z, half ^ (dom % 2)

        return pairs(move)

    return dict(
        side=pairs(lambda x, c, z, y: (x, c, z, 1 - y)),
        near=pairs(lambda x, c, z, y: (x, c, z ^ 1, y)),
        inward=pairs(lambda x, c, z, y: {0: (x, c, 1, y), 3: (x, c, 2, y)}.get(z)),
        outward=pairs(lambda x, c, z, y: {1: (x, c, 0, y), 2: (x, c, 3, y)}.get(z)),
        cross=pairs(lambda x, c, z, y: {1: (x, c, 2, y), 2: (x, c, 1, y)}.get(z)),
        up=ring(1),
        down=ring(-1),
    )


def swapped(pairs):
    return [(target, source) for source, target in pairs]


def relay_shards(bg, jit, inverse_variance, measured, adjacent, tier):
    moves = relay_permutations()

    def send(array, name):
        return lax.ppermute(array, AXES, moves[name])

    rows, cells = bg.shape
    members = rows * lax.axis_size("mem")
    half_chunks = cells // 2 // CHUNK
    dom, mem = lax.axis_index("dom"), lax.axis_index("mem")
    core, z, y = dom % 2, mem // 2, mem % 2
    inner = jnp.logical_or(z == 1, z == 2)
    half = jnp.bitwise_xor(y, core)
    halves = jnp.stack([1 - half, half]).astype(jnp.int32)
    role = jnp.stack([y, inner]).astype(jnp.int32)

    def in_order(low_first, mine, other):
        return jnp.concatenate(
            [jnp.where(low_first, mine, other), jnp.where(low_first, other, mine)], axis=0
        )

    def after(value, *others):
        return lax.optimization_barrier((value, others))[0]

    gain = gain_of(inverse_variance, measured)[None, :]
    last = half_chunks - 1
    order = [last, *range(last)]
    groups = []
    for size in GROUPS:
        groups.append(order[:size])
        order = order[size:]
    assert not order and all(groups)
    count = len(groups)
    sides, home = [], []
    for size in SIDE_GROUPS:
        taken = groups[len(home) : len(home) + size]
        first = 0
        for group in taken:
            home.append((len(sides), first))
            first += len(group)
        sides.append([chunk for group in taken for chunk in group])

    first_chunks = jnp.array(sides[0], jnp.int32)
    away, own = first_source(
        halves[:, None] * half_chunks + first_chunks[None, :],
        measured,
        bg,
        jit,
        inverse_variance[None, :],
    )
    came = [send(away, "side")]
    owns = [own]
    pieces = source(sides[1:], after(halves, away), bg, jit, gain)
    token = after(role, pieces[0][0])
    came.append(send(after(pieces[0][0], away), "side"))
    owns += [piece[1] for piece in pieces]
    table = after(dense_weights(adjacent, tier, members), token)

    packed = {}
    finished = []
    todo = list(range(half_chunks))
    outer, across = [], []
    worked, going_out, going_back = [], [], []

    def parts(t):
        number, first = home[t]
        places = [first + i for i in range(len(groups[t]))]
        return [[tile(array[number], k, 2 * rows) for k in places] for array in (owns, came)]

    def outer_states(t):
        return [tile(outer[t], 2 * i, 2 * rows) for i in range(len(groups[t]))]

    def take_back():
        nonlocal token
        for chunks, inc, back, other in going_back:
            token = after(token, other)
            finished.append((chunks, inc, back, other))
        going_back.clear()

    def send_on(items):
        nonlocal token
        for chunks, inc, back in items:
            back = after(back, token)
            pairs = [part.reshape(len(chunks), 2, rows, CHUNK)[:, 1] for part in (inc, back)]
            other = jnp.where(inner, *pairs).reshape(-1, CHUNK)
            token = after(token, other)
            going_back.append((chunks, inc, back, send(other, "side")))

    def work(t):
        nonlocal token
        mine, others = parts(t)
        ahead = len(groups[t + 1]) if t + 1 < count else 0
        chunks = center(
            token,
            [
                [mine[i], others[i]]
                + [tile(outer[t], 2 * i, 2 * rows), tile(outer[t], 2 * i + 1, 2 * rows)]
                + [tile(across[t], i, 2 * rows), tile(across[t + 1], ahead + i, 2 * rows)]
                for i in range(len(mine))
            ],
        )
        packed.update(zip(groups[t], chunks))
        token = after(role, chunks[0])
        ready = [i for i in todo if all(j in packed for j in (i - 1, i, i + 1))]
        while ready:
            n = 1
            while n < MOST and t < count - 2 and ready[0] + n in ready:
                n += 1
            now, ready = ready[:n], ready[n:]
            if t == count - 1 and len(going_out) > 2:
                token = after(token, going_out[-3][2])
            window = [packed[i] for i in range(now[0] - 1, now[-1] + 2)]
            inc, inc_outer = update(token, window, weights, now[0])
            for i in now:
                todo.remove(i)
            token = after(role, inc)
            worked.append((now, inc, inc_outer))
            if t >= count - 2:
                send_out()

    def send_out():
        for now, inc, inc_outer in worked:
            going_out.append((now, inc, send(after(inc_outer, token), "outward")))
        worked.clear()

    for t in range(count + 1):
        if t == 0:
            side_table = send(table, "side")
        if t == 1:
            token = after(token, side_table)
            table = in_order(y == 0, table, side_table)
            near_table = send(table, "near")
        if t == 2:
            token = after(token, near_table)
            table = in_order(z % 2 == 0, table, near_table)
            far_table = send(table, "cross")
        if t == 3:
            token = after(token, far_table)
            weights = jnp.transpose(jnp.where(half == z // 2, table, far_table))
        if t > 0:
            token = after(token, outer[t - 1], across[t - 1])
        if t == 4:
            token = after(token, packed[-1])
        if t == 5:
            token = after(token, packed[last + 1])
        if t < count:
            states, cross = collect(token, *parts(t), outer_states(t - 1) if t else [])
            outer.append(send(states, "inward"))
            if t + 1 < len(SIDE_GROUPS) and t + 1 >= len(came):
                came.append(send(after(pieces[t][0], cross), "side"))
        else:
            older = outer[t - 1].reshape(-1, 2, 2 * rows, CHUNK)
            cross = older[:, 0].reshape(-1, CHUNK)
        token = after(role, cross)
        across.append(send(cross, "cross"))
        send_out()
        take_back()
        ending = len(going_out)
        if t >= 2:
            work(t - 2)
        send_on(going_out[:ending])
        del going_out[:ending]
        if t == 2:
            packed[-1] = send(after(packed[last], token), "up")
        if t == 3:
            packed[last + 1] = send(after(packed[0], token), "down")
    token = after(token, across[count])
    work(count - 1)
    send_on(going_out)
    take_back()
    return assemble(jnp.append(role, half), finished, half_chunks)


def with_halo(block, sides, width):
    for axis, dim in sides:
        count = lax.axis_size(axis)
        forward = [(i, (i + 1) % count) for i in range(count)]
        low = lax.ppermute(
            lax.slice_in_dim(block, block.shape[dim] - width, None, axis=dim), axis, forward
        )
        high = lax.ppermute(
            lax.slice_in_dim(block, 0, width, axis=dim), axis, swapped(forward)
        )
        block = jnp.concatenate([low, block, high], axis=dim)
    return block


def gathered_shards(bg, jit, inverse_variance, measured, adjacent, tier):
    rim_cells = REACH * PC
    gain = gain_of(inverse_variance, measured)
    residual = (
        gain[None, :] * (jit.astype(jnp.float32) - bg.astype(jnp.float32))
    ).astype(jnp.bfloat16)
    states = lax.all_to_all(bg, "mem", split_axis=1, concat_axis=0, tiled=True)
    innov_local = lax.all_to_all(residual, "mem", split_axis=1, concat_axis=0, tiled=True)
    mean = jnp.mean(states.astype(jnp.float32), axis=0)
    draws_local = (states.astype(jnp.float32) - mean[None, :]).astype(jnp.bfloat16)
    padded = with_halo(jnp.stack((draws_local, innov_local)), ((AXES, 2),), rim_cells)
    draws, innov = padded[0], padded[1]
    members = draws.shape[0]
    local_cells = draws.shape[1] - 2 * rim_cells
    local_patches = local_cells // PC
    table = dense_weights(adjacent, tier, members)
    block_size = math.gcd(local_patches, 8)
    window_patches = block_size + 2 * REACH

    def update_block(counter, increment):
        start = counter * block_size
        own = lax.dynamic_slice_in_dim(draws, (REACH + start) * PC, block_size * PC, 1)
        window = lax.dynamic_slice_in_dim(draws, start * PC, window_patches * PC, 1)
        window_innov = lax.dynamic_slice_in_dim(innov, start * PC, window_patches * PC, 1)
        rows = lax.dynamic_slice_in_dim(table, start, block_size, 0)
        weights = jnp.stack(
            [jnp.pad(rows[a], (a, block_size - 1 - a)) for a in range(block_size)]
        )
        covariance = lax.dot_general(
            own, window, (((0,), (0,)), ((), ())), preferred_element_type=jnp.float32
        )
        covariance = covariance.reshape(block_size, PC, window_patches, PC)
        covariance = (covariance * weights[:, None, :, None]).astype(jnp.bfloat16)
        result = lax.dot_general(
            window_innov,
            covariance.reshape(block_size * PC, window_patches * PC),
            (((1,), (1,)), ((), ())),
            preferred_element_type=jnp.float32,
        )
        return lax.dynamic_update_slice_in_dim(
            increment, result.astype(jnp.bfloat16), start * PC, 1
        )

    increment = jnp.zeros((members, local_cells), jnp.bfloat16)
    increment = lax.fori_loop(0, local_patches // block_size, update_block, increment)
    return lax.all_to_all(increment, "mem", split_axis=0, concat_axis=1, tiled=True)


def solution(mesh):
    in_specs = (
        P("mem", "dom"),
        P("mem", "dom"),
        P("dom"),
        P("dom"),
        P(AXES, None),
        P(AXES, None),
    )
    across = mesh.shape["dom"] // 2
    line = mesh.shape["mem"] // across
    shards = relay_shards if (across, line) == (2, 4) else gathered_shards
    return jax.shard_map(
        shards, mesh=mesh, in_specs=in_specs, out_specs=P("mem", "dom"), check_vma=False
    )
```

```python
import functools
import math

import jax
import jax.numpy as jnp
from jax import lax
from jax.experimental import pallas as pl
from jax.experimental.pallas import tpu as pltpu
from jax.sharding import PartitionSpec as P

PC = 64
REACH = 16
NCLASS = 8
AXES = ("dom", "mem")
CHUNK = REACH * PC
BLOCK = 256
BLOCK_PATCHES = BLOCK // PC
BLOCKS = CHUNK // BLOCK
WINDOW_PATCHES = BLOCK_PATCHES + 2 * REACH
VMEM_BYTES = 24 * 2**20
GROUPS = (1, 2, 3, 2, 2, 1, 1)
MOST = 3
SIDE_GROUPS = (1, 1, 1, 4)


def gc_taper(taper_cutoff_length):
    return (
        1.0
        - 5.0 / 3.0 * taper_cutoff_length**2
        + 0.625 * taper_cutoff_length**3
        + 0.5 * taper_cutoff_length**4
        - 0.25 * taper_cutoff_length**5
    )


def gain_of(measurement_inverse_variance, measured_point_number):
    observed = (jnp.arange(PC, dtype=jnp.int32)[None, :] < measured_point_number[:, None]).reshape(
        -1
    )
    return jnp.where(observed, measurement_inverse_variance, jnp.float32(0.0))


def dense_weights(adjacent_region_list, nearby_separation_tier, all_members):
    rows = adjacent_region_list.shape[0]
    groups = lax.axis_size("mem")
    all_patches = rows * lax.axis_size("dom") * groups
    first = (lax.axis_index("dom") * groups + lax.axis_index("mem")) * rows
    own_ids = first + jnp.arange(rows, dtype=jnp.int32)[:, None]
    offset = (
        adjacent_region_list - own_ids + all_patches + all_patches // 2
    ) % all_patches - all_patches // 2
    weight = gc_taper(nearby_separation_tier.astype(jnp.float32) / NCLASS) / (all_members - 1)
    slots = jnp.arange(2 * REACH + 1, dtype=jnp.int32) - REACH
    return jnp.sum(
        jnp.where(offset[:, :, None] == slots[None, None, :], weight[:, :, None], 0.0), axis=1
    )


def whole(array):
    return array, pl.BlockSpec(memory_space=pltpu.VMEM)


def tile(array, number, rows):
    return array, pl.BlockSpec((rows, CHUNK), lambda *_: (number, 0))


def on_one_step(kernel, scalars, inputs, outputs, name, scratch=()):
    inputs, specs = zip(*inputs)
    return pl.pallas_call(
        kernel,
        grid=(1,),
        in_specs=[pl.BlockSpec(memory_space=pltpu.SMEM)] * len(scalars) + list(specs),
        out_specs=[whole(a)[1] for a in outputs],
        out_shape=list(outputs),
        scratch_shapes=list(scratch),
        cost_estimate=pl.CostEstimate(flops=1024, bytes_accessed=1024, transcendentals=0),
        compiler_params=pltpu.CompilerParams(vmem_limit_bytes=VMEM_BYTES),
        name=name,
    )(*scalars, *inputs)


def shape_of(rows, cells):
    return jax.ShapeDtypeStruct((rows, cells), jnp.bfloat16)


def source_rows(bg, jit, gain, piece):
    rows = bg.shape[0]
    piece[pl.ds(0, rows), :] = bg
    piece[pl.ds(rows, rows), :] = (
        gain * (jit.astype(jnp.float32) - bg.astype(jnp.float32))
    ).astype(jnp.bfloat16)


def gain_row(inverse_variance, measured, first):
    cell = lax.broadcasted_iota(jnp.int32, (1, CHUNK), 1)
    number = jnp.zeros((1, CHUNK), jnp.int32)
    for patch in range(CHUNK // PC):
        number = jnp.where(cell // PC == patch, measured[first + patch], number)
    return jnp.where(cell % PC < number, inverse_variance, 0.0)


def first_source_kernel(place, measured, bg1, jit1, var1, bg2, jit2, var2, piece1, piece2):
    for piece, bg, jit, var, out in ((0, bg1, jit1, var1, piece1), (1, bg2, jit2, var2, piece2)):
        first = place[piece, pl.program_id(0)] * (CHUNK // PC)
        source_rows(bg[...], jit[...], gain_row(var[...], measured, first), out)


def first_source(place, measured, bg, jit, inverse_variance):
    rows, n = bg.shape[0], place.shape[1]

    def specs(piece):
        return [
            pl.BlockSpec((size, CHUNK), lambda i, place, _: (0, place[piece, i]))
            for size in (rows, rows, 1)
        ]

    out = shape_of(2 * rows * n, CHUNK)
    return pl.pallas_call(
        first_source_kernel,
        grid_spec=pltpu.PrefetchScalarGridSpec(
            num_scalar_prefetch=2,
            grid=(n,),
            in_specs=specs(0) + specs(1),
            out_specs=[pl.BlockSpec((2 * rows, CHUNK), lambda i, place, _: (i, 0))] * 2,
        ),
        out_shape=(out, out),
        cost_estimate=pl.CostEstimate(flops=1024, bytes_accessed=1024, transcendentals=0),
        name="first_source",
    )(place, measured, bg, jit, inverse_variance, bg, jit, inverse_variance)


def source_kernel(groups, halves, bg, jit, gain, *pieces):
    half = bg.shape[1] // 2
    rows = 2 * bg.shape[0]
    for side in range(2):
        for group, piece in zip(groups, pieces[side::2]):
            for j, chunk in enumerate(group):
                at = pl.ds(pl.multiple_of(halves[side] * half + chunk * CHUNK, CHUNK), CHUNK)
                source_rows(bg[:, at], jit[:, at], gain[:, at], piece.at[pl.ds(j * rows, rows)])


def source(groups, halves, bg, jit, gain):
    rows = 2 * bg.shape[0]
    outputs = [shape_of(rows * len(group), CHUNK) for group in groups for _ in range(2)]
    inputs = [whole(a) for a in (bg, jit, gain)]
    pieces = on_one_step(
        functools.partial(source_kernel, groups), [halves], inputs, outputs, "source"
    )
    return list(zip(pieces[::2], pieces[1::2]))


def collect_kernel(n, role, *refs):
    own, came, older, (both, across) = refs[:n], refs[n : 2 * n], refs[2 * n : -2], refs[-2:]
    for i in range(n):
        rows = own[i].shape[0] // 2
        for k, part in enumerate((own[i], came[i])):
            both[pl.ds((4 * i + k) * rows, rows), :] = part[pl.ds(0, rows), :]
            both[pl.ds((4 * i + 2 + k) * rows, rows), :] = part[pl.ds(rows, rows), :]
            across[pl.ds((2 * i + k) * rows, rows), :] = part[pl.ds(0, rows), :]
    for i, part in enumerate(older):
        across[pl.ds((n + i) * part.shape[0], part.shape[0]), :] = part[...]


def collect(role, own, came, older):
    n, rows = len(own), own[0][1].block_shape[0]
    outputs = [shape_of(2 * rows * n, CHUNK), shape_of(rows * (n + len(older)), CHUNK)]
    return on_one_step(
        functools.partial(collect_kernel, n), [role], [*own, *came, *older], outputs, "collect"
    )


def center_kernel(role, own, came, outer, outer_innov, across, across_outer, out):
    rows = own.shape[0] // 2
    low = pl.multiple_of(role[0] * rows, rows)
    high = pl.multiple_of((1 - role[0]) * rows, rows)
    own_first = role[0] == 0
    members, lanes = 8 * rows, out.shape[1]

    def in_turn(row, cells):
        mine, other = own[pl.ds(row, rows), cells], came[pl.ds(row, rows), cells]
        return [jnp.where(own_first, mine, other), jnp.where(own_first, other, mine)]

    for j in range(CHUNK // BLOCK):
        cells = pl.ds(j * BLOCK, BLOCK)
        parts = in_turn(0, cells)
        parts += [ref[pl.ds(at, rows), cells] for ref in (outer, across, across_outer) for at in (low, high)]
        parts = [part.astype(jnp.float32) for part in parts]
        total = functools.reduce(jnp.add, parts)
        mean = jnp.sum(total, axis=0, keepdims=True) / members
        perturb = jnp.concatenate([(p - mean).astype(jnp.bfloat16) for p in parts], axis=0)
        out[cells, :] = perturb.T
    for j in range(CHUNK // lanes):
        cells = pl.ds(j * lanes, lanes)
        parts = in_turn(rows, cells) + [outer_innov[pl.ds(at, rows), cells] for at in (low, high)]
        for k, part in enumerate(parts):
            out[pl.ds(CHUNK + (4 * j + k) * rows, rows), :] = part


def centers_kernel(role, *refs):
    n = len(refs) // 7

    @pl.when(role[1] != 0)
    def _():
        for i in range(n):
            center_kernel(role, *refs[6 * i : 6 * i + 6], refs[6 * n + i])


def center(role, chunks):
    rows = chunks[0][0][1].block_shape[0] // 2
    lanes = 8 * rows
    outputs = [shape_of(CHUNK + 4 * rows * (CHUNK // lanes), lanes)] * len(chunks)
    inputs = [part for chunk in chunks for part in chunk]
    return on_one_step(centers_kernel, [role], inputs, outputs, "center")


def window_pieces(b):
    return [(0, b * BLOCK, CHUNK - b * BLOCK), (1, 0, CHUNK), (2, 0, (b + 1) * BLOCK)]


def split_pieces(pieces, lanes):
    for chunk, first, cells in pieces:
        while cells:
            some = min(cells, lanes - first % lanes)
            yield chunk, first, some
            first, cells = first + some, cells - some


def update_kernel(n, first_chunk, role, *refs):
    packed, (weights, inner, outer, covariance) = refs[: n + 2], refs[n + 2 :]
    lanes = packed[0].shape[1]
    rows = lanes // 8
    low, high = role[0] * rows, (1 - role[0]) * rows

    patch = lax.broadcasted_iota(jnp.int32, (WINDOW_PATCHES, BLOCK), 1) // PC

    def covariances(k):
        i, b = divmod(k, BLOCKS)
        own = packed[i + 1][pl.ds(b * BLOCK, BLOCK), :]
        spread = None
        for a in range(BLOCK_PATCHES):
            column = (first_chunk * BLOCKS + k) * BLOCK_PATCHES + a
            shifted = jnp.concatenate(
                [jnp.zeros((size, 1), jnp.float32) for size in (a,) if size]
                + [weights[:, column : column + 1]]
                + [jnp.zeros((size, 1), jnp.float32) for size in (BLOCK_PATCHES - 1 - a,) if size]
            )
            spread = shifted if spread is None else jnp.where(patch >= a, shifted, spread)
        done = 0
        for chunk, first, cells in window_pieces(b):
            patches = cells // PC
            product = lax.dot_general(
                packed[i + chunk][pl.ds(first, cells), :],
                own,
                (((1,), (1,)), ((), ())),
                preferred_element_type=jnp.float32,
            )
            weight = spread[done : done + patches]
            product = product.reshape(patches, PC, BLOCK) * weight[:, None, :]
            covariance[k % 2, pl.ds(done * PC, cells), :] = product.astype(jnp.bfloat16).reshape(
                cells, BLOCK
            )
            done += patches

    def increments(k):
        i, b = divmod(k, BLOCKS)
        total, done = None, 0
        for chunk, first, cells in split_pieces(window_pieces(b), lanes):
            j, lane = divmod(first, lanes)
            term = jnp.dot(
                packed[i + chunk][pl.ds(CHUNK + 4 * j * rows, 4 * rows), pl.ds(lane, cells)],
                covariance[k % 2, pl.ds(done, cells), :],
                preferred_element_type=jnp.float32,
            )
            total = term if total is None else total + term
            done += cells
        total = total.astype(jnp.bfloat16)
        cells = pl.ds(b * BLOCK, BLOCK)
        for out, at in ((inner, 0), (outer, 2 * rows)):
            for place, first in ((low, at), (high, at + rows)):
                place = pl.multiple_of(2 * i * rows + place, rows)
                out[pl.ds(place, rows), cells] = total[first : first + rows]

    @pl.when(role[1] != 0)
    def _():
        for k in range(n * BLOCKS + 1):
            if k < n * BLOCKS:
                covariances(k)
            if k > 0:
                increments(k - 1)


def update(role, packed, weights, first_chunk):
    n = len(packed) - 2
    members = packed[0].shape[1]
    rows = members // 8
    out = shape_of(2 * rows * n, CHUNK)
    window = WINDOW_PATCHES * PC
    return on_one_step(
        functools.partial(update_kernel, n, first_chunk),
        [role],
        [whole(a) for a in (*packed, weights)],
        [out, out],
        "update",
        scratch=[pltpu.VMEM((2, window, BLOCK), jnp.bfloat16)],
    )


def assemble_kernel(groups, half_chunks, role, *refs):
    out = refs[-1]
    rows = out.shape[0]

    def cells(half, chunk):
        first = half * (half_chunks * CHUNK) + chunk * CHUNK
        return pl.ds(pl.multiple_of(first, CHUNK), CHUNK)

    for k, group in enumerate(groups):
        inc, back, other = refs[3 * k : 3 * k + 3]
        for i, chunk in enumerate(group):
            out[:, cells(1 - role[2], chunk)] = other[pl.ds(i * rows, rows), :]
            for inner, mine in ((1, inc), (0, back)):

                @pl.when(role[1] == inner)
                def _():
                    out[:, cells(role[2], chunk)] = mine[pl.ds(2 * i * rows, rows), :]


def assemble(role, finished, half_chunks):
    groups = [tuple(chunks) for chunks, *_ in finished]
    inputs = [whole(part) for _, *parts in finished for part in parts]
    rows = finished[0][3].shape[0] // len(groups[0])
    out = shape_of(rows, 2 * half_chunks * CHUNK)
    return pl.pallas_call(
        functools.partial(assemble_kernel, groups, half_chunks),
        grid=(1,),
        in_specs=[pl.BlockSpec(memory_space=pltpu.SMEM)] + [spec for _, spec in inputs],
        out_specs=pl.BlockSpec(out.shape, lambda *_: (0, 0)),
        out_shape=out,
        cost_estimate=pl.CostEstimate(flops=1024, bytes_accessed=1024, transcendentals=0),
        compiler_params=pltpu.CompilerParams(vmem_limit_bytes=VMEM_BYTES),
        name="assemble",
    )(role, *[array for array, _ in inputs])


def relay_permutations():
    devices = [
        (x, c, z, y) for x in range(2) for c in range(2) for z in range(4) for y in range(2)
    ]

    def number(x, c, z, y):
        return (x * 2 + c) * 8 + z * 2 + y

    def pairs(move):
        moves = [(device, move(*device)) for device in devices]
        return [(number(*a), number(*b)) for a, b in moves if b is not None]

    def ring(step):
        def move(x, c, z, y):
            if z not in (1, 2):
                return None
            segment = (2 * (2 * x + c) + (y ^ c) + step) % 8
            dom, half = divmod(segment, 2)
            return dom // 2, dom % 2, z, half ^ (dom % 2)

        return pairs(move)

    return dict(
        side=pairs(lambda x, c, z, y: (x, c, z, 1 - y)),
        near=pairs(lambda x, c, z, y: (x, c, z ^ 1, y)),
        inward=pairs(lambda x, c, z, y: {0: (x, c, 1, y), 3: (x, c, 2, y)}.get(z)),
        outward=pairs(lambda x, c, z, y: {1: (x, c, 0, y), 2: (x, c, 3, y)}.get(z)),
        cross=pairs(lambda x, c, z, y: {1: (x, c, 2, y), 2: (x, c, 1, y)}.get(z)),
        up=ring(1),
        down=ring(-1),
    )


def swapped(pairs):
    return [(target, source) for source, target in pairs]


def relay_shards(bg, jit, inverse_variance, measured, adjacent, tier):
    moves = relay_permutations()

    def send(array, name):
        return lax.ppermute(array, AXES, moves[name])

    rows, cells = bg.shape
    members = rows * lax.axis_size("mem")
    half_chunks = cells // 2 // CHUNK
    dom, mem = lax.axis_index("dom"), lax.axis_index("mem")
    core, z, y = dom % 2, mem // 2, mem % 2
    inner = jnp.logical_or(z == 1, z == 2)
    half = jnp.bitwise_xor(y, core)
    halves = jnp.stack([1 - half, half]).astype(jnp.int32)
    role = jnp.stack([y, inner]).astype(jnp.int32)

    def in_order(low_first, mine, other):
        return jnp.concatenate(
            [jnp.where(low_first, mine, other), jnp.where(low_first, other, mine)], axis=0
        )

    def after(value, *others):
        return lax.optimization_barrier((value, others))[0]

    gain = gain_of(inverse_variance, measured)[None, :]
    last = half_chunks - 1
    order = [last, *range(last)]
    groups = []
    for size in GROUPS:
        groups.append(order[:size])
        order = order[size:]
    assert not order and all(groups)
    count = len(groups)
    sides, home = [], []
    for size in SIDE_GROUPS:
        taken = groups[len(home) : len(home) + size]
        first = 0
        for group in taken:
            home.append((len(sides), first))
            first += len(group)
        sides.append([chunk for group in taken for chunk in group])

    first_chunks = jnp.array(sides[0], jnp.int32)
    away, own = first_source(
        halves[:, None] * half_chunks + first_chunks[None, :],
        measured,
        bg,
        jit,
        inverse_variance[None, :],
    )
    came = [send(away, "side")]
    owns = [own]
    pieces = source(sides[1:], after(halves, away), bg, jit, gain)
    token = after(role, pieces[0][0])
    came.append(send(after(pieces[0][0], away), "side"))
    owns += [piece[1] for piece in pieces]
    table = after(dense_weights(adjacent, tier, members), token)

    packed = {}
    finished = []
    todo = list(range(half_chunks))
    outer, across = [], []
    worked, going_out, going_back = [], [], []

    def parts(t):
        number, first = home[t]
        places = [first + i for i in range(len(groups[t]))]
        return [[tile(array[number], k, 2 * rows) for k in places] for array in (owns, came)]

    def outer_states(t):
        return [tile(outer[t], 2 * i, 2 * rows) for i in range(len(groups[t]))]

    def take_back():
        nonlocal token
        for chunks, inc, back, other in going_back:
            token = after(token, other)
            finished.append((chunks, inc, back, other))
        going_back.clear()

    def send_on(items):
        nonlocal token
        for chunks, inc, back in items:
            back = after(back, token)
            pairs = [part.reshape(len(chunks), 2, rows, CHUNK)[:, 1] for part in (inc, back)]
            other = jnp.where(inner, *pairs).reshape(-1, CHUNK)
            token = after(token, other)
            going_back.append((chunks, inc, back, send(other, "side")))

    def work(t):
        nonlocal token
        mine, others = parts(t)
        ahead = len(groups[t + 1]) if t + 1 < count else 0
        chunks = center(
            token,
            [
                [mine[i], others[i]]
                + [tile(outer[t], 2 * i, 2 * rows), tile(outer[t], 2 * i + 1, 2 * rows)]
                + [tile(across[t], i, 2 * rows), tile(across[t + 1], ahead + i, 2 * rows)]
                for i in range(len(mine))
            ],
        )
        packed.update(zip(groups[t], chunks))
        token = after(role, chunks[0])
        ready = [i for i in todo if all(j in packed for j in (i - 1, i, i + 1))]
        while ready:
            n = 1
            while n < MOST and t < count - 2 and ready[0] + n in ready:
                n += 1
            now, ready = ready[:n], ready[n:]
            if t == count - 1 and len(going_out) > 2:
                token = after(token, going_out[-3][2])
            window = [packed[i] for i in range(now[0] - 1, now[-1] + 2)]
            inc, inc_outer = update(token, window, weights, now[0])
            for i in now:
                todo.remove(i)
            token = after(role, inc)
            worked.append((now, inc, inc_outer))
            if t >= count - 2:
                send_out()

    def send_out():
        for now, inc, inc_outer in worked:
            going_out.append((now, inc, send(after(inc_outer, token), "outward")))
        worked.clear()

    for t in range(count + 1):
        if t == 0:
            side_table = send(table, "side")
        if t == 1:
            token = after(token, side_table)
            table = in_order(y == 0, table, side_table)
            near_table = send(table, "near")
        if t == 2:
            token = after(token, near_table)
            table = in_order(z % 2 == 0, table, near_table)
            far_table = send(table, "cross")
        if t == 3:
            token = after(token, far_table)
            weights = jnp.transpose(jnp.where(half == z // 2, table, far_table))
        if t > 0:
            token = after(token, outer[t - 1], across[t - 1])
        if t == 4:
            token = after(token, packed[-1])
        if t == 5:
            token = after(token, packed[last + 1])
        if t < count:
            states, cross = collect(token, *parts(t), outer_states(t - 1) if t else [])
            outer.append(send(states, "inward"))
            if t + 1 < len(SIDE_GROUPS) and t + 1 >= len(came):
                came.append(send(after(pieces[t][0], cross), "side"))
        else:
            older = outer[t - 1].reshape(-1, 2, 2 * rows, CHUNK)
            cross = older[:, 0].reshape(-1, CHUNK)
        token = after(role, cross)
        across.append(send(cross, "cross"))
        send_out()
        ending = len(going_out)
        if t >= 2:
            work(t - 2)
        take_back()
        send_on(going_out[:ending])
        del going_out[:ending]
        if t == 2:
            packed[-1] = send(after(packed[last], token), "up")
        if t == 3:
            packed[last + 1] = send(after(packed[0], token), "down")
    token = after(token, across[count])
    work(count - 1)
    send_on(going_out)
    take_back()
    return assemble(jnp.append(role, half), finished, half_chunks)


def with_halo(block, sides, width):
    for axis, dim in sides:
        count = lax.axis_size(axis)
        forward = [(i, (i + 1) % count) for i in range(count)]
        low = lax.ppermute(
            lax.slice_in_dim(block, block.shape[dim] - width, None, axis=dim), axis, forward
        )
        high = lax.ppermute(
            lax.slice_in_dim(block, 0, width, axis=dim), axis, swapped(forward)
        )
        block = jnp.concatenate([low, block, high], axis=dim)
    return block


def gathered_shards(bg, jit, inverse_variance, measured, adjacent, tier):
    rim_cells = REACH * PC
    gain = gain_of(inverse_variance, measured)
    residual = (
        gain[None, :] * (jit.astype(jnp.float32) - bg.astype(jnp.float32))
    ).astype(jnp.bfloat16)
    states = lax.all_to_all(bg, "mem", split_axis=1, concat_axis=0, tiled=True)
    innov_local = lax.all_to_all(residual, "mem", split_axis=1, concat_axis=0, tiled=True)
    mean = jnp.mean(states.astype(jnp.float32), axis=0)
    draws_local = (states.astype(jnp.float32) - mean[None, :]).astype(jnp.bfloat16)
    padded = with_halo(jnp.stack((draws_local, innov_local)), ((AXES, 2),), rim_cells)
    draws, innov = padded[0], padded[1]
    members = draws.shape[0]
    local_cells = draws.shape[1] - 2 * rim_cells
    local_patches = local_cells // PC
    table = dense_weights(adjacent, tier, members)
    block_size = math.gcd(local_patches, 8)
    window_patches = block_size + 2 * REACH

    def update_block(counter, increment):
        start = counter * block_size
        own = lax.dynamic_slice_in_dim(draws, (REACH + start) * PC, block_size * PC, 1)
        window = lax.dynamic_slice_in_dim(draws, start * PC, window_patches * PC, 1)
        window_innov = lax.dynamic_slice_in_dim(innov, start * PC, window_patches * PC, 1)
        rows = lax.dynamic_slice_in_dim(table, start, block_size, 0)
        weights = jnp.stack(
            [jnp.pad(rows[a], (a, block_size - 1 - a)) for a in range(block_size)]
        )
        covariance = lax.dot_general(
            own, window, (((0,), (0,)), ((), ())), preferred_element_type=jnp.float32
        )
        covariance = covariance.reshape(block_size, PC, window_patches, PC)
        covariance = (covariance * weights[:, None, :, None]).astype(jnp.bfloat16)
        result = lax.dot_general(
            window_innov,
            covariance.reshape(block_size * PC, window_patches * PC),
            (((1,), (1,)), ((), ())),
            preferred_element_type=jnp.float32,
        )
        return lax.dynamic_update_slice_in_dim(
            increment, result.astype(jnp.bfloat16), start * PC, 1
        )

    increment = jnp.zeros((members, local_cells), jnp.bfloat16)
    increment = lax.fori_loop(0, local_patches // block_size, update_block, increment)
    return lax.all_to_all(increment, "mem", split_axis=0, concat_axis=1, tiled=True)


def solution(mesh):
    in_specs = (
        P("mem", "dom"),
        P("mem", "dom"),
        P("dom"),
        P("dom"),
        P(AXES, None),
        P(AXES, None),
    )
    across = mesh.shape["dom"] // 2
    line = mesh.shape["mem"] // across
    shards = relay_shards if (across, line) == (2, 4) else gathered_shards
    return jax.shard_map(
        shards, mesh=mesh, in_specs=in_specs, out_specs=P("mem", "dom"), check_vma=False
    )
```

```python
import functools
import math

import jax
import jax.numpy as jnp
from jax import lax
from jax.experimental import pallas as pl
from jax.experimental.pallas import tpu as pltpu
from jax.sharding import PartitionSpec as P

PC = 64
REACH = 16
NCLASS = 8
AXES = ("dom", "mem")
CHUNK = REACH * PC
BLOCK = 256
BLOCK_PATCHES = BLOCK // PC
BLOCKS = CHUNK // BLOCK
WINDOW_PATCHES = BLOCK_PATCHES + 2 * REACH
VMEM_BYTES = 24 * 2**20
GROUPS = (1, 2, 3, 2, 2, 1, 1)
MOST = 3
SIDE_GROUPS = (1, 1, 1, 4)


def gc_taper(taper_cutoff_length):
    return (
        1.0
        - 5.0 / 3.0 * taper_cutoff_length**2
        + 0.625 * taper_cutoff_length**3
        + 0.5 * taper_cutoff_length**4
        - 0.25 * taper_cutoff_length**5
    )


def gain_of(measurement_inverse_variance, measured_point_number):
    observed = (jnp.arange(PC, dtype=jnp.int32)[None, :] < measured_point_number[:, None]).reshape(
        -1
    )
    return jnp.where(observed, measurement_inverse_variance, jnp.float32(0.0))


def dense_weights(adjacent_region_list, nearby_separation_tier, all_members):
    rows = adjacent_region_list.shape[0]
    groups = lax.axis_size("mem")
    all_patches = rows * lax.axis_size("dom") * groups
    first = (lax.axis_index("dom") * groups + lax.axis_index("mem")) * rows
    own_ids = first + jnp.arange(rows, dtype=jnp.int32)[:, None]
    offset = (
        adjacent_region_list - own_ids + all_patches + all_patches // 2
    ) % all_patches - all_patches // 2
    weight = gc_taper(nearby_separation_tier.astype(jnp.float32) / NCLASS) / (all_members - 1)
    slots = jnp.arange(2 * REACH + 1, dtype=jnp.int32) - REACH
    return jnp.sum(
        jnp.where(offset[:, :, None] == slots[None, None, :], weight[:, :, None], 0.0), axis=1
    )


def whole(array):
    return array, pl.BlockSpec(memory_space=pltpu.VMEM)


def tile(array, number, rows):
    return array, pl.BlockSpec((rows, CHUNK), lambda *_: (number, 0))


def on_one_step(kernel, scalars, inputs, outputs, name, scratch=()):
    inputs, specs = zip(*inputs)
    return pl.pallas_call(
        kernel,
        grid=(1,),
        in_specs=[pl.BlockSpec(memory_space=pltpu.SMEM)] * len(scalars) + list(specs),
        out_specs=[whole(a)[1] for a in outputs],
        out_shape=list(outputs),
        scratch_shapes=list(scratch),
        cost_estimate=pl.CostEstimate(flops=1024, bytes_accessed=1024, transcendentals=0),
        compiler_params=pltpu.CompilerParams(vmem_limit_bytes=VMEM_BYTES),
        name=name,
    )(*scalars, *inputs)


def shape_of(rows, cells):
    return jax.ShapeDtypeStruct((rows, cells), jnp.bfloat16)


def source_rows(bg, jit, gain, piece):
    rows = bg.shape[0]
    piece[pl.ds(0, rows), :] = bg
    piece[pl.ds(rows, rows), :] = (
        gain * (jit.astype(jnp.float32) - bg.astype(jnp.float32))
    ).astype(jnp.bfloat16)


def gain_row(inverse_variance, measured, first):
    cell = lax.broadcasted_iota(jnp.int32, (1, CHUNK), 1)
    number = jnp.zeros((1, CHUNK), jnp.int32)
    for patch in range(CHUNK // PC):
        number = jnp.where(cell // PC == patch, measured[first + patch], number)
    return jnp.where(cell % PC < number, inverse_variance, 0.0)


def first_source_kernel(place, measured, bg1, jit1, var1, bg2, jit2, var2, piece1, piece2):
    for piece, bg, jit, var, out in ((0, bg1, jit1, var1, piece1), (1, bg2, jit2, var2, piece2)):
        first = place[piece, pl.program_id(0)] * (CHUNK // PC)
        source_rows(bg[...], jit[...], gain_row(var[...], measured, first), out)


def first_source(place, measured, bg, jit, inverse_variance):
    rows, n = bg.shape[0], place.shape[1]

    def specs(piece):
        return [
            pl.BlockSpec((size, CHUNK), lambda i, place, _: (0, place[piece, i]))
            for size in (rows, rows, 1)
        ]

    out = shape_of(2 * rows * n, CHUNK)
    return pl.pallas_call(
        first_source_kernel,
        grid_spec=pltpu.PrefetchScalarGridSpec(
            num_scalar_prefetch=2,
            grid=(n,),
            in_specs=specs(0) + specs(1),
            out_specs=[pl.BlockSpec((2 * rows, CHUNK), lambda i, place, _: (i, 0))] * 2,
        ),
        out_shape=(out, out),
        cost_estimate=pl.CostEstimate(flops=1024, bytes_accessed=1024, transcendentals=0),
        name="first_source",
    )(place, measured, bg, jit, inverse_variance, bg, jit, inverse_variance)


def source_kernel(groups, halves, bg, jit, gain, *pieces):
    half = bg.shape[1] // 2
    rows = 2 * bg.shape[0]
    for side in range(2):
        for group, piece in zip(groups, pieces[side::2]):
            for j, chunk in enumerate(group):
                at = pl.ds(pl.multiple_of(halves[side] * half + chunk * CHUNK, CHUNK), CHUNK)
                source_rows(bg[:, at], jit[:, at], gain[:, at], piece.at[pl.ds(j * rows, rows)])


def source(groups, halves, bg, jit, gain):
    rows = 2 * bg.shape[0]
    outputs = [shape_of(rows * len(group), CHUNK) for group in groups for _ in range(2)]
    inputs = [whole(a) for a in (bg, jit, gain)]
    pieces = on_one_step(
        functools.partial(source_kernel, groups), [halves], inputs, outputs, "source"
    )
    return list(zip(pieces[::2], pieces[1::2]))


def collect_kernel(n, role, *refs):
    own, came, older, (both, across) = refs[:n], refs[n : 2 * n], refs[2 * n : -2], refs[-2:]
    for i in range(n):
        rows = own[i].shape[0] // 2
        for k, part in enumerate((own[i], came[i])):
            both[pl.ds((4 * i + k) * rows, rows), :] = part[pl.ds(0, rows), :]
            both[pl.ds((4 * i + 2 + k) * rows, rows), :] = part[pl.ds(rows, rows), :]
            across[pl.ds((2 * i + k) * rows, rows), :] = part[pl.ds(0, rows), :]
    for i, part in enumerate(older):
        across[pl.ds((n + i) * part.shape[0], part.shape[0]), :] = part[...]


def collect(role, own, came, older):
    n, rows = len(own), own[0][1].block_shape[0]
    outputs = [shape_of(2 * rows * n, CHUNK), shape_of(rows * (n + len(older)), CHUNK)]
    return on_one_step(
        functools.partial(collect_kernel, n), [role], [*own, *came, *older], outputs, "collect"
    )


def center_kernel(role, own, came, outer, outer_innov, across, across_outer, out):
    rows = own.shape[0] // 2
    low = pl.multiple_of(role[0] * rows, rows)
    high = pl.multiple_of((1 - role[0]) * rows, rows)
    own_first = role[0] == 0
    members, lanes = 8 * rows, out.shape[1]

    def in_turn(row, cells):
        mine, other = own[pl.ds(row, rows), cells], came[pl.ds(row, rows), cells]
        return [jnp.where(own_first, mine, other), jnp.where(own_first, other, mine)]

    for j in range(CHUNK // BLOCK):
        cells = pl.ds(j * BLOCK, BLOCK)
        parts = in_turn(0, cells)
        parts += [ref[pl.ds(at, rows), cells] for ref in (outer, across, across_outer) for at in (low, high)]
        parts = [part.astype(jnp.float32) for part in parts]
        total = functools.reduce(jnp.add, parts)
        mean = jnp.sum(total, axis=0, keepdims=True) / members
        perturb = jnp.concatenate([(p - mean).astype(jnp.bfloat16) for p in parts], axis=0)
        out[cells, :] = perturb.T
    for j in range(CHUNK // lanes):
        cells = pl.ds(j * lanes, lanes)
        parts = in_turn(rows, cells) + [outer_innov[pl.ds(at, rows), cells] for at in (low, high)]
        for k, part in enumerate(parts):
            out[pl.ds(CHUNK + (4 * j + k) * rows, rows), :] = part


def centers_kernel(role, *refs):
    n = len(refs) // 7

    @pl.when(role[1] != 0)
    def _():
        for i in range(n):
            center_kernel(role, *refs[6 * i : 6 * i + 6], refs[6 * n + i])


def center(role, chunks):
    rows = chunks[0][0][1].block_shape[0] // 2
    lanes = 8 * rows
    outputs = [shape_of(CHUNK + 4 * rows * (CHUNK // lanes), lanes)] * len(chunks)
    inputs = [part for chunk in chunks for part in chunk]
    return on_one_step(centers_kernel, [role], inputs, outputs, "center")


def window_pieces(b):
    return [(0, b * BLOCK, CHUNK - b * BLOCK), (1, 0, CHUNK), (2, 0, (b + 1) * BLOCK)]


def split_pieces(pieces, lanes):
    for chunk, first, cells in pieces:
        while cells:
            some = min(cells, lanes - first % lanes)
            yield chunk, first, some
            first, cells = first + some, cells - some


def update_kernel(n, first_chunk, role, *refs):
    packed, (weights, inner, outer, covariance) = refs[: n + 2], refs[n + 2 :]
    lanes = packed[0].shape[1]
    rows = lanes // 8
    low, high = role[0] * rows, (1 - role[0]) * rows

    patch = lax.broadcasted_iota(jnp.int32, (WINDOW_PATCHES, BLOCK), 1) // PC

    def covariances(k):
        i, b = divmod(k, BLOCKS)
        own = packed[i + 1][pl.ds(b * BLOCK, BLOCK), :]
        spread = None
        for a in range(BLOCK_PATCHES):
            column = (first_chunk * BLOCKS + k) * BLOCK_PATCHES + a
            shifted = jnp.concatenate(
                [jnp.zeros((size, 1), jnp.float32) for size in (a,) if size]
                + [weights[:, column : column + 1]]
                + [jnp.zeros((size, 1), jnp.float32) for size in (BLOCK_PATCHES - 1 - a,) if size]
            )
            spread = shifted if spread is None else jnp.where(patch >= a, shifted, spread)
        done = 0
        for chunk, first, cells in window_pieces(b):
            patches = cells // PC
            product = lax.dot_general(
                packed[i + chunk][pl.ds(first, cells), :],
                own,
                (((1,), (1,)), ((), ())),
                preferred_element_type=jnp.float32,
            )
            weight = spread[done : done + patches]
            product = product.reshape(patches, PC, BLOCK) * weight[:, None, :]
            covariance[k % 2, pl.ds(done * PC, cells), :] = product.astype(jnp.bfloat16).reshape(
                cells, BLOCK
            )
            done += patches

    def increments(k):
        i, b = divmod(k, BLOCKS)
        total, done = None, 0
        for chunk, first, cells in split_pieces(window_pieces(b), lanes):
            j, lane = divmod(first, lanes)
            term = jnp.dot(
                packed[i + chunk][pl.ds(CHUNK + 4 * j * rows, 4 * rows), pl.ds(lane, cells)],
                covariance[k % 2, pl.ds(done, cells), :],
                preferred_element_type=jnp.float32,
            )
            total = term if total is None else total + term
            done += cells
        total = total.astype(jnp.bfloat16)
        cells = pl.ds(b * BLOCK, BLOCK)
        for out, at in ((inner, 0), (outer, 2 * rows)):
            for place, first in ((low, at), (high, at + rows)):
                place = pl.multiple_of(2 * i * rows + place, rows)
                out[pl.ds(place, rows), cells] = total[first : first + rows]

    @pl.when(role[1] != 0)
    def _():
        for k in range(n * BLOCKS + 1):
            if k < n * BLOCKS:
                covariances(k)
            if k > 0:
                increments(k - 1)


def update(role, packed, weights, first_chunk):
    n = len(packed) - 2
    members = packed[0].shape[1]
    rows = members // 8
    out = shape_of(2 * rows * n, CHUNK)
    window = WINDOW_PATCHES * PC
    return on_one_step(
        functools.partial(update_kernel, n, first_chunk),
        [role],
        [whole(a) for a in (*packed, weights)],
        [out, out],
        "update",
        scratch=[pltpu.VMEM((2, window, BLOCK), jnp.bfloat16)],
    )


def assemble_kernel(groups, half_chunks, role, *refs):
    out = refs[-1]
    rows = out.shape[0]

    def cells(half, chunk):
        first = half * (half_chunks * CHUNK) + chunk * CHUNK
        return pl.ds(pl.multiple_of(first, CHUNK), CHUNK)

    for k, group in enumerate(groups):
        inc, back, other = refs[3 * k : 3 * k + 3]
        for i, chunk in enumerate(group):
            out[:, cells(1 - role[2], chunk)] = other[pl.ds(i * rows, rows), :]
            for inner, mine in ((1, inc), (0, back)):

                @pl.when(role[1] == inner)
                def _():
                    out[:, cells(role[2], chunk)] = mine[pl.ds(2 * i * rows, rows), :]


def assemble(role, finished, half_chunks):
    groups = [tuple(chunks) for chunks, *_ in finished]
    inputs = [whole(part) for _, *parts in finished for part in parts]
    rows = finished[0][3].shape[0] // len(groups[0])
    out = shape_of(rows, 2 * half_chunks * CHUNK)
    return pl.pallas_call(
        functools.partial(assemble_kernel, groups, half_chunks),
        grid=(1,),
        in_specs=[pl.BlockSpec(memory_space=pltpu.SMEM)] + [spec for _, spec in inputs],
        out_specs=pl.BlockSpec(out.shape, lambda *_: (0, 0)),
        out_shape=out,
        cost_estimate=pl.CostEstimate(flops=1024, bytes_accessed=1024, transcendentals=0),
        compiler_params=pltpu.CompilerParams(vmem_limit_bytes=VMEM_BYTES),
        name="assemble",
    )(role, *[array for array, _ in inputs])


def relay_permutations():
    devices = [
        (x, c, z, y) for x in range(2) for c in range(2) for z in range(4) for y in range(2)
    ]

    def number(x, c, z, y):
        return (x * 2 + c) * 8 + z * 2 + y

    def pairs(move):
        moves = [(device, move(*device)) for device in devices]
        return [(number(*a), number(*b)) for a, b in moves if b is not None]

    def ring(step):
        def move(x, c, z, y):
            if z not in (1, 2):
                return None
            segment = (2 * (2 * x + c) + (y ^ c) + step) % 8
            dom, half = divmod(segment, 2)
            return dom // 2, dom % 2, z, half ^ (dom % 2)

        return pairs(move)

    return dict(
        side=pairs(lambda x, c, z, y: (x, c, z, 1 - y)),
        near=pairs(lambda x, c, z, y: (x, c, z ^ 1, y)),
        inward=pairs(lambda x, c, z, y: {0: (x, c, 1, y), 3: (x, c, 2, y)}.get(z)),
        outward=pairs(lambda x, c, z, y: {1: (x, c, 0, y), 2: (x, c, 3, y)}.get(z)),
        cross=pairs(lambda x, c, z, y: {1: (x, c, 2, y), 2: (x, c, 1, y)}.get(z)),
        up=ring(1),
        down=ring(-1),
    )


def swapped(pairs):
    return [(target, source) for source, target in pairs]


def relay_shards(bg, jit, inverse_variance, measured, adjacent, tier):
    moves = relay_permutations()

    def send(array, name):
        return lax.ppermute(array, AXES, moves[name])

    rows, cells = bg.shape
    members = rows * lax.axis_size("mem")
    half_chunks = cells // 2 // CHUNK
    dom, mem = lax.axis_index("dom"), lax.axis_index("mem")
    core, z, y = dom % 2, mem // 2, mem % 2
    inner = jnp.logical_or(z == 1, z == 2)
    half = jnp.bitwise_xor(y, core)
    halves = jnp.stack([1 - half, half]).astype(jnp.int32)
    role = jnp.stack([y, inner]).astype(jnp.int32)

    def in_order(low_first, mine, other):
        return jnp.concatenate(
            [jnp.where(low_first, mine, other), jnp.where(low_first, other, mine)], axis=0
        )

    def after(value, *others):
        return lax.optimization_barrier((value, others))[0]

    gain = gain_of(inverse_variance, measured)[None, :]
    last = half_chunks - 1
    order = [last, *range(last)]
    groups = []
    for size in GROUPS:
        groups.append(order[:size])
        order = order[size:]
    assert not order and all(groups)
    count = len(groups)
    sides, home = [], []
    for size in SIDE_GROUPS:
        taken = groups[len(home) : len(home) + size]
        first = 0
        for group in taken:
            home.append((len(sides), first))
            first += len(group)
        sides.append([chunk for group in taken for chunk in group])

    first_chunks = jnp.array(sides[0], jnp.int32)
    away, own = first_source(
        halves[:, None] * half_chunks + first_chunks[None, :],
        measured,
        bg,
        jit,
        inverse_variance[None, :],
    )
    came = [send(away, "side")]
    owns = [own]
    pieces = source(sides[1:], after(halves, away), bg, jit, gain)
    token = after(role, pieces[0][0])
    came.append(send(after(pieces[0][0], away), "side"))
    owns += [piece[1] for piece in pieces]
    table = after(dense_weights(adjacent, tier, members), token)

    packed = {}
    finished = []
    todo = list(range(half_chunks))
    outer, across = [], []
    worked, going_out, going_back = [], [], []

    def parts(t):
        number, first = home[t]
        places = [first + i for i in range(len(groups[t]))]
        return [[tile(array[number], k, 2 * rows) for k in places] for array in (owns, came)]

    def outer_states(t):
        return [tile(outer[t], 2 * i, 2 * rows) for i in range(len(groups[t]))]

    def take_back():
        nonlocal token
        for chunks, inc, back, other in going_back:
            token = after(token, other)
            finished.append((chunks, inc, back, other))
        going_back.clear()

    def send_on(items):
        nonlocal token
        for chunks, inc, back in items:
            back = after(back, token)
            pairs = [part.reshape(len(chunks), 2, rows, CHUNK)[:, 1] for part in (inc, back)]
            other = jnp.where(inner, *pairs).reshape(-1, CHUNK)
            token = after(token, other)
            going_back.append((chunks, inc, back, send(other, "side")))

    def work(t):
        nonlocal token
        mine, others = parts(t)
        ahead = len(groups[t + 1]) if t + 1 < count else 0
        chunks = center(
            token,
            [
                [mine[i], others[i]]
                + [tile(outer[t], 2 * i, 2 * rows), tile(outer[t], 2 * i + 1, 2 * rows)]
                + [tile(across[t], i, 2 * rows), tile(across[t + 1], ahead + i, 2 * rows)]
                for i in range(len(mine))
            ],
        )
        packed.update(zip(groups[t], chunks))
        token = after(role, chunks[0])
        ready = [i for i in todo if all(j in packed for j in (i - 1, i, i + 1))]
        while ready:
            n = 1
            most = 2 if t == count - 3 else MOST
            while n < most and t < count - 2 and ready[0] + n in ready:
                n += 1
            now, ready = ready[:n], ready[n:]
            if t == count - 1 and len(going_out) > 2:
                token = after(token, going_out[-3][2])
            window = [packed[i] for i in range(now[0] - 1, now[-1] + 2)]
            inc, inc_outer = update(token, window, weights, now[0])
            for i in now:
                todo.remove(i)
            token = after(role, inc)
            worked.append((now, inc, inc_outer))
            if t == count - 3 and ready:
                token = after(token, outer[-1])
            if t >= count - 2:
                send_out()

    def send_out():
        for now, inc, inc_outer in worked:
            going_out.append((now, inc, send(after(inc_outer, token), "outward")))
        worked.clear()

    for t in range(count + 1):
        if t == 0:
            side_table = send(table, "side")
        if t == 1:
            token = after(token, side_table)
            table = in_order(y == 0, table, side_table)
            near_table = send(table, "near")
        if t == 2:
            token = after(token, near_table)
            table = in_order(z % 2 == 0, table, near_table)
            far_table = send(table, "cross")
        if t == 3:
            token = after(token, far_table)
            weights = jnp.transpose(jnp.where(half == z // 2, table, far_table))
        if t > 0:
            token = after(token, outer[t - 1], across[t - 1])
        if t == 4:
            token = after(token, packed[-1])
        if t == 5:
            token = after(token, packed[last + 1])
        if t < count:
            states, cross = collect(token, *parts(t), outer_states(t - 1) if t else [])
            outer.append(send(states, "inward"))
            if t + 1 < len(SIDE_GROUPS) and t + 1 >= len(came):
                came.append(send(after(pieces[t][0], cross), "side"))
        else:
            older = outer[t - 1].reshape(-1, 2, 2 * rows, CHUNK)
            cross = older[:, 0].reshape(-1, CHUNK)
        token = after(role, cross)
        across.append(send(cross, "cross"))
        send_out()
        ending = len(going_out)
        if t >= 2:
            work(t - 2)
        take_back()
        send_on(going_out[:ending])
        del going_out[:ending]
        if t == 2:
            packed[-1] = send(after(packed[last], token), "up")
        if t == 3:
            packed[last + 1] = send(after(packed[0], token), "down")
    token = after(token, across[count])
    work(count - 1)
    send_on(going_out)
    take_back()
    return assemble(jnp.append(role, half), finished, half_chunks)


def with_halo(block, sides, width):
    for axis, dim in sides:
        count = lax.axis_size(axis)
        forward = [(i, (i + 1) % count) for i in range(count)]
        low = lax.ppermute(
            lax.slice_in_dim(block, block.shape[dim] - width, None, axis=dim), axis, forward
        )
        high = lax.ppermute(
            lax.slice_in_dim(block, 0, width, axis=dim), axis, swapped(forward)
        )
        block = jnp.concatenate([low, block, high], axis=dim)
    return block


def gathered_shards(bg, jit, inverse_variance, measured, adjacent, tier):
    rim_cells = REACH * PC
    gain = gain_of(inverse_variance, measured)
    residual = (
        gain[None, :] * (jit.astype(jnp.float32) - bg.astype(jnp.float32))
    ).astype(jnp.bfloat16)
    states = lax.all_to_all(bg, "mem", split_axis=1, concat_axis=0, tiled=True)
    innov_local = lax.all_to_all(residual, "mem", split_axis=1, concat_axis=0, tiled=True)
    mean = jnp.mean(states.astype(jnp.float32), axis=0)
    draws_local = (states.astype(jnp.float32) - mean[None, :]).astype(jnp.bfloat16)
    padded = with_halo(jnp.stack((draws_local, innov_local)), ((AXES, 2),), rim_cells)
    draws, innov = padded[0], padded[1]
    members = draws.shape[0]
    local_cells = draws.shape[1] - 2 * rim_cells
    local_patches = local_cells // PC
    table = dense_weights(adjacent, tier, members)
    block_size = math.gcd(local_patches, 8)
    window_patches = block_size + 2 * REACH

    def update_block(counter, increment):
        start = counter * block_size
        own = lax.dynamic_slice_in_dim(draws, (REACH + start) * PC, block_size * PC, 1)
        window = lax.dynamic_slice_in_dim(draws, start * PC, window_patches * PC, 1)
        window_innov = lax.dynamic_slice_in_dim(innov, start * PC, window_patches * PC, 1)
        rows = lax.dynamic_slice_in_dim(table, start, block_size, 0)
        weights = jnp.stack(
            [jnp.pad(rows[a], (a, block_size - 1 - a)) for a in range(block_size)]
        )
        covariance = lax.dot_general(
            own, window, (((0,), (0,)), ((), ())), preferred_element_type=jnp.float32
        )
        covariance = covariance.reshape(block_size, PC, window_patches, PC)
        covariance = (covariance * weights[:, None, :, None]).astype(jnp.bfloat16)
        result = lax.dot_general(
            window_innov,
            covariance.reshape(block_size * PC, window_patches * PC),
            (((1,), (1,)), ((), ())),
            preferred_element_type=jnp.float32,
        )
        return lax.dynamic_update_slice_in_dim(
            increment, result.astype(jnp.bfloat16), start * PC, 1
        )

    increment = jnp.zeros((members, local_cells), jnp.bfloat16)
    increment = lax.fori_loop(0, local_patches // block_size, update_block, increment)
    return lax.all_to_all(increment, "mem", split_axis=0, concat_axis=1, tiled=True)


def solution(mesh):
    in_specs = (
        P("mem", "dom"),
        P("mem", "dom"),
        P("dom"),
        P("dom"),
        P(AXES, None),
        P(AXES, None),
    )
    across = mesh.shape["dom"] // 2
    line = mesh.shape["mem"] // across
    shards = relay_shards if (across, line) == (2, 4) else gathered_shards
    return jax.shard_map(
        shards, mesh=mesh, in_specs=in_specs, out_specs=P("mem", "dom"), check_vma=False
    )
```
